32 devices in a mesh: ens: 4 (over y, x), tile: 8 (over z, core).
Axes of the slice: x: 2, y: 2, z: 4, core: 2. Of those that a mesh axis runs over, the one named last changes fastest.
Arguments:
- surface: float32 [8192, 1024], P(('ens', 'tile')), parts along dimension 0, may hold values from -6 to 6
- flux_x: float32 [8192, 1024], P(('ens', 'tile')), parts along dimension 0, may hold values from -3 to 3
- flux_y: float32 [8192, 1024], P(('ens', 'tile')), parts along dimension 0, may hold values from -3 to 3
- celerity: float32 [8192, 1024], P(('ens', 'tile')), parts along dimension 0, may hold values from 0.05 to 0.45
- bed_depth: float32 [8192, 1024], P(('ens', 'tile')), parts along dimension 0, may hold values from 0.2 to 3
- roughness: float32 [8192, 1024], P(('ens', 'tile')), parts along dimension 0, may hold values from 0.2 to 2
- smoother: bfloat16 [256, 256], replicated, may hold values from -0.5 to 1.5
- block_plan: int32 [32, 4], P(('ens', 'tile')), parts along dimension 0, may hold values from 0 to 3, as said below
Outputs:
- new_surface: float32 [8192, 1024], P(('ens', 'tile')), parts along dimension 0
- new_flux_x: float32 [8192, 1024], P(('ens', 'tile')), parts along dimension 0
- new_flux_y: float32 [8192, 1024], P(('ens', 'tile')), parts along dimension 0
- resident: float32 [96, 2, 256, 256], P(('ens', 'tile')), parts along dimension 0
- energy: float32 [8], P('ens'), parts along dimension 0
The draws below stay inside these ranges and needn't reach their ends.
There are 4 independent parts, one for each index of `ens`. The reference program is written for one: setup_inputs(seed, part) draws one part's arguments, and reference() takes and returns one part's arrays. A program takes and returns all parts, laid end to end along the dimension named above; an argument that names none is the same for every part. Nothing has to cross between parts.
Inputs may be any that keep to these rules, and one draw needn't show every extreme that they name: `block_plan`: codes per block: 0 dry, 1 to 3 wet with the slots of the steps. Every tile holds exactly one block of each code 1, 2 and 3 and one dry block, so every slot holds exactly one block.
All inputs are finite; a program needn't handle non-finite values.
Results may differ from the reference program's by a relative error of at most 0.022.
Values may be sent and summed in bfloat16 or wider, within the bound.
A program may use at most 64 MiB of HBM per device.

```python
import math
import jax
import jax.numpy as jnp
from jax import lax

B = 256
BPD = 4
STEPS = 2
SUB = 12
RSLOT = 3
NC = 1024
NX = 2048
N_TILE = 8


def draw_smoother(key, part):
    noise = jax.random.normal(key, (B, B), jnp.float32)
    return (jnp.eye(B, dtype=jnp.float32) + noise * (0.3 / math.sqrt(B))).astype(jnp.bfloat16)


def draw_block_plan(key, part):
    spots = jnp.arange(BPD, dtype=jnp.int32)
    scores = jax.random.randint(key, (N_TILE, BPD), 0, 2 ** 20) * BPD + spots[None, :]
    ranks = jnp.argsort(scores, axis=1).astype(jnp.int32)
    codes = jnp.where(ranks < 4, ranks, 0).astype(jnp.int32)
    return codes.astype(jnp.int32)


def level_of(own_key, dims, split, low, largest):
    def one(dim, blocks):
        steps = jax.random.uniform(jax.random.fold_in(jax.random.fold_in(own_key, 6), dim), (blocks,), jnp.float32, low / len(split), largest / len(split))
        return jnp.repeat(jnp.exp(steps), dims[dim] // blocks).reshape((-1,) + (1,) * (len(dims) - dim - 1))

    factor_of = one(*split[0])
    for cut in split[1:]:
        factor_of = factor_of * one(*cut)
    return factor_of


def scatter_about(key, shape, deviation, reach, cuts=(), kind=jnp.bfloat16):
    drawn = jax.random.normal(key, shape, jnp.float32) * deviation
    if len(cuts) > 0:
        drawn = level_of(key, shape, cuts, -0.22, 0.18) * drawn
    return jnp.clip(drawn, min=-reach, max=reach).astype(kind)


def setup_inputs(seed: int = 0, part: int = 0) -> dict:
    splits = jax.random.split(jax.random.key(seed), 9)
    part_splits = jax.random.split(jax.random.fold_in(splits[8], part), 9)
    return {
        "surface": scatter_about(part_splits[0], (NX, NC), 1.0, 6.0, ((0, 8),), jnp.float32),
        "flux_x": scatter_about(part_splits[1], (NX, NC), 0.5, 3.0, ((0, 8),), jnp.float32),
        "flux_y": scatter_about(part_splits[2], (NX, NC), 0.5, 3.0, ((0, 8),), jnp.float32),
        "celerity": jnp.clip(jnp.exp(math.log(0.45) - 2.1972245 * jax.random.uniform(part_splits[3], (NX, NC), jnp.float32) ** level_of(part_splits[3], (NX, NC), ((0, 8),), -0.2, 0.2)), 0.05, 0.45),
        "bed_depth": jnp.clip(0.2 + 2.8 * jax.random.uniform(part_splits[4], (NX, NC), jnp.float32) ** level_of(part_splits[4], (NX, NC), ((0, 8),), -0.2, 0.2), 0.2, 3.0),
        "roughness": jnp.clip(jnp.exp(math.log(2.0) - 2.3025851 * jax.random.uniform(part_splits[5], (NX, NC), jnp.float32) ** level_of(part_splits[5], (NX, NC), ((0, 8),), -0.2, 0.2)), 0.2, 2.0),
        "smoother": draw_smoother(jax.random.fold_in(splits[8], 71), part),
        "block_plan": draw_block_plan(jax.random.fold_in(jax.random.fold_in(splits[8], part), 71), part),
    }


def to_blocks(field, tiles):
    return field.reshape(tiles, B, BPD, B).transpose(0, 2, 1, 3).reshape(tiles * BPD, B, B)


def from_blocks(blocks, tiles):
    return blocks.reshape(tiles, BPD, B, B).transpose(0, 2, 1, 3).reshape(tiles * B, BPD * B)


def settle_slot(held, drag_ratio, smoother):
    weight = drag_ratio.astype(jnp.float32)
    wide = smoother.astype(jnp.float32)
    settled = jnp.zeros(held.shape, jnp.float32)
    for _ in range(SUB):
        partial_rows = jnp.einsum("fij,kj->fik", held.astype(jnp.float32), wide).astype(jnp.bfloat16)
        mixed_full = jnp.einsum("ki,fij->fkj", wide, partial_rows.astype(jnp.float32))
        settled = mixed_full / (1.0 + weight * jnp.abs(mixed_full))
        held = settled.astype(jnp.bfloat16)
    return settled


def reference(surface, flux_x, flux_y, celerity, bed_depth, roughness, smoother, block_plan):
    row_total, col_total = surface.shape
    tiles = row_total // B
    half_cols = col_total // 2
    col_ids = jnp.arange(col_total, dtype=jnp.int32)
    right_edge = (col_ids % half_cols == half_cols - 1)[None, :]
    left_edge = (col_ids % half_cols == 0)[None, :]
    level, flow_x, flow_y = surface, flux_x, flux_y
    zero_row = jnp.zeros((1, col_total), jnp.float32)
    wet_flags = (block_plan > 0).reshape(-1)
    tile_ids = jnp.arange(tiles, dtype=jnp.int32)[:, None]
    dest_slot = (block_plan - 1).astype(jnp.int32)
    dest_tile = (tile_ids + dest_slot) % tiles
    target = (dest_tile * RSLOT + dest_slot).reshape(-1).astype(jnp.int32)
    slot_ids = jnp.arange(tiles * RSLOT, dtype=jnp.int32)
    block_ids = jnp.arange(tiles * BPD, dtype=jnp.int32)
    matches = (target[:, None] == slot_ids[None, :]) & wet_flags[:, None]
    source = jnp.sum(jnp.where(matches, block_ids[:, None], 0), axis=0).astype(jnp.int32)
    filled = jnp.any(matches, axis=0)
    safe_target = jnp.where(wet_flags, target, 0).astype(jnp.int32)

    def settle_pair(pair):
        return settle_slot(pair[0], pair[1], smoother)

    resident = jnp.zeros((tiles * RSLOT, 2, B, B), jnp.float32)
    for repeat in range(STEPS):
        ahead_rows = jnp.concatenate([level[1:], zero_row], 0)
        flow_x = flow_x - celerity * (ahead_rows - level)
        right_cells = jnp.where(right_edge, 0.0, jnp.roll(level, -1, axis=1))
        flow_y = flow_y - celerity * (right_cells - level)
        behind_x = jnp.concatenate([zero_row, flow_x[:-1]], 0)
        behind_y = jnp.where(left_edge, 0.0, jnp.roll(flow_y, 1, axis=1))
        level = level - (flow_x - behind_x) - (flow_y - behind_y)
        drag_full = (roughness / jnp.maximum(level + bed_depth, 1.0)).astype(jnp.bfloat16)
        flow_blocks = jnp.stack([to_blocks(flow_x, tiles), to_blocks(flow_y, tiles)], 1)
        drag_blocks = to_blocks(drag_full, tiles)
        held = jnp.where(filled[:, None, None, None], flow_blocks[source], 0.0).astype(jnp.bfloat16)
        drag_held = jnp.where(filled[:, None, None], drag_blocks[source], jnp.zeros((), drag_blocks.dtype))
        resident = lax.map(settle_pair, (held, drag_held))
        updated = jnp.where(wet_flags[:, None, None, None], resident[safe_target], flow_blocks)
        flow_x = from_blocks(updated[:, 0], tiles)
        flow_y = from_blocks(updated[:, 1], tiles)
    row_weight = 1.0 + 2.0 * jnp.arange(row_total, dtype=jnp.float32) / row_total
    squares = (row_weight[:, None] * level * level).reshape(row_total, 2, half_cols)
    energy = jnp.sum(squares, axis=(0, 2)) / (row_total * half_cols)
    return level, flow_x, flow_y, resident, energy
```

```python
import functools

import jax
import jax.numpy as jnp
from jax import lax
from jax.experimental import pallas as pl
from jax.experimental.pallas import tpu as pltpu
from jax.sharding import PartitionSpec as P

STEPS = 2
SUB = 12
STRIP = 16
MESH = pl.DeviceIdType.MESH


def window_kernel(
    n, plan, s_ref, surface_in, flux_x_in, flux_y_in, celerity_in, bed_in, rough_in,
    level_out, held_out, got_out, energy_out,
    level, flux_x, flux_y, celerity, bed, rough, drag, turned, held, settled,
    below, above_level, above_flux, above_celerity, shares,
    load_sem, store_sem, send_sem, recv_sem, share_send, share_recv,
):
    rows, cols = flux_y.shape
    side = s_ref.shape[0]
    blocks = cols // side
    half = cols // 2
    me = lax.axis_index("tile")
    ahead_tile = lax.rem(me + 1, n)
    behind_tile = lax.rem(me + n - 1, n)
    top = me == 0
    bottom = me == n - 1
    f32, bf16 = jnp.float32, jnp.bfloat16

    loads = [
        pltpu.make_async_copy(source, target, load_sem.at[i])
        for i, (source, target) in enumerate(
            (
                (surface_in, level.at[pl.ds(0, rows)]),
                (celerity_in, celerity),
                (flux_x_in, flux_x.at[pl.ds(8, rows)]),
                (flux_y_in, flux_y),
                (bed_in, bed),
                (rough_in, rough),
            )
        )
    ]
    for load in loads:
        load.start()

    barrier = pltpu.get_barrier_semaphore()

    def greet(d, _):
        pl.semaphore_signal(barrier, inc=1, device_id={"tile": lax.rem(me + d, n)}, device_id_type=MESH)
        return 0

    lax.fori_loop(1, n, greet, 0)
    pl.semaphore_wait(barrier, n - 1)

    def remote(source, target, index, device):
        return pltpu.make_async_remote_copy(
            src_ref=source, dst_ref=target, send_sem=send_sem.at[index], recv_sem=recv_sem.at[index],
            device_id={"tile": device}, device_id_type=MESH,
        )

    last = pl.ds(rows - 8, 8)
    up = [
        remote(surface_in.at[pl.ds(0, 8)], below.at[0], 0, behind_tile),
        remote(level.at[pl.ds(0, 8)], below.at[1], 1, behind_tile),
    ]
    down = [
        [
            remote(surface_in.at[last], above_level.at[0], 2, ahead_tile),
            remote(flux_x_in.at[last], above_flux.at[0], 3, ahead_tile),
            remote(celerity_in.at[last], above_celerity, 4, ahead_tile),
        ],
        [
            remote(level.at[last], above_level.at[1], 5, ahead_tile),
            remote(flux_x.at[pl.ds(rows, 8)], above_flux.at[1], 6, ahead_tile),
        ],
    ]

    @pl.when(jnp.logical_not(top))
    def _():
        up[0].start()

    @pl.when(jnp.logical_not(bottom))
    def _():
        for copy in down[0]:
            copy.start()

    turned[...] = s_ref[...].astype(f32).T.astype(bf16)
    codes = [plan[0, c] for c in range(blocks)]

    def choose(options, matches):
        chosen = options[0]
        for option, match in zip(options[1:], matches[1:]):
            chosen = jnp.where(match, option, chosen)
        return chosen

    def with_code(wide, code):
        parts = [wide[:, c * side : (c + 1) * side] for c in range(blocks)]
        return choose(parts, [codes[c] == code for c in range(blocks)])

    def joined(which, at, size):
        options = [settled[code, which, pl.ds(at, size), :] for code in range(4)]
        return jnp.concatenate(
            [choose(options, [codes[c] == code for code in range(4)]) for c in range(blocks)], 1
        )

    col_ids = lax.broadcasted_iota(jnp.int32, (1, cols), 1)
    right_edge = lax.rem(col_ids, half) == half - 1
    left_edge = lax.rem(col_ids, half) == 0

    for load in loads:
        load.wait()

    def strip_flux(step, which, at):
        if step == 0:
            return flux_x[pl.ds(8 + at, STRIP)] if which == 0 else flux_y[pl.ds(at, STRIP)]
        return joined(which, at, STRIP)

    def advance(step):
        @pl.when(bottom)
        def _():
            level[pl.ds(rows, 8)] = jnp.zeros((8, cols), f32)

        @pl.when(jnp.logical_not(bottom))
        def _():
            up[step].wait_recv()
            level[pl.ds(rows, 8)] = below[step]

        @pl.when(top)
        def _():
            flux_x[pl.ds(0, 8)] = jnp.zeros((8, cols), f32)

        @pl.when(jnp.logical_not(top))
        def _():
            for copy in down[step]:
                copy.wait_recv()
            flux_x[pl.ds(0, 8)] = above_flux[step] - above_celerity[...] * (
                level[0:1] - above_level[step]
            )

        def strip(i, _):
            at = pl.multiple_of(i * STRIP, STRIP)
            now = level[pl.ds(at, STRIP)]
            after = level[pl.ds(at + STRIP, 8)]
            ahead = pltpu.roll(jnp.concatenate([now, after], 0), STRIP + 7, 0)[:STRIP]
            wave = celerity[pl.ds(at, STRIP)]
            new_x = strip_flux(step, 0, at) - wave * (ahead - now)
            right = jnp.where(right_edge, 0.0, pltpu.roll(now, cols - 1, 1))
            new_y = strip_flux(step, 1, at) - wave * (right - now)
            behind_x = pltpu.roll(jnp.concatenate([flux_x[pl.ds(at, 8)], new_x], 0), 1, 0)[8:]
            behind_y = jnp.where(left_edge, 0.0, pltpu.roll(new_y, 1, 1))
            new_level = now - (new_x - behind_x) - (new_y - behind_y)
            flux_x[pl.ds(8 + at, STRIP)] = new_x
            level[pl.ds(at, STRIP)] = new_level
            ratio = rough[pl.ds(at, STRIP)] / jnp.maximum(new_level + bed[pl.ds(at, STRIP)], 1.0)
            ratio = ratio.astype(bf16).astype(f32)
            for code in range(1, 4):
                drag[code - 1, pl.ds(at, STRIP), :] = with_code(ratio, code)
            for which, new in enumerate((new_x, new_y)):
                for code in range(4):
                    mine = with_code(new, code)
                    held[code, which, pl.ds(at, STRIP), :] = mine.astype(bf16)
                    if code == 0:
                        settled[0, which, pl.ds(at, STRIP), :] = mine
            return 0

        lax.fori_loop(0, rows // STRIP, strip, 0)

    def settle(wanted):
        def once(code, which):
            mixed = jnp.dot(held[code, which], turned[...], preferred_element_type=f32).astype(bf16)
            smoothed = jnp.dot(s_ref[...], mixed, preferred_element_type=f32)
            weight = drag[code - 1]
            return smoothed * pl.reciprocal(1.0 + weight * jnp.abs(smoothed), approx=True)

        def body(i, _):
            for code in wanted:
                for which in range(2):
                    held[code, which] = once(code, which).astype(bf16)
            return 0

        lax.fori_loop(0, SUB - 1, body, 0)
        for code in wanted:
            for which in range(2):
                value = once(code, which)
                settled[code, which] = value
                held[code, which] = value.astype(bf16)

    advance(0)
    for copy, edge in ((up[0], top), (down[0][0], bottom), (down[0][1], bottom), (down[0][2], bottom)):
        @pl.when(jnp.logical_not(edge))
        def _():
            copy.wait_send()

    @pl.when(jnp.logical_not(top))
    def _():
        up[1].start()

    @pl.when(jnp.logical_not(bottom))
    def _():
        down[1][0].start()

    settle((1, 2, 3))
    flux_x[pl.ds(rows, 8)] = joined(0, rows - 8, 8)

    @pl.when(jnp.logical_not(top))
    def _():
        up[1].wait_send()

    @pl.when(jnp.logical_not(bottom))
    def _():
        down[1][1].start()
        down[1][0].wait_send()
        down[1][1].wait_send()

    advance(1)

    total = n * rows

    def add_up(i, sums):
        at = pl.multiple_of(i * 8, 8)
        row = (me * rows + at + lax.broadcasted_iota(jnp.int32, (8, 1), 0)).astype(f32)
        value = level[pl.ds(at, 8)]
        return sums + (1.0 + 2.0 * row / total) * (value * value)

    sums = lax.fori_loop(0, rows // 8, add_up, jnp.zeros((8, cols), f32))
    for scenario in range(2):
        share = jnp.zeros((8, 128), f32)
        for c in range(half // 128):
            share = share + sums[:, scenario * half + c * 128 : scenario * half + (c + 1) * 128]
        shares[me, scenario] = share

    def spread(d, _):
        share_copy(d).start()
        return 0

    def share_copy(d):
        return pltpu.make_async_remote_copy(
            src_ref=shares.at[me], dst_ref=shares.at[me],
            send_sem=share_send.at[d - 1], recv_sem=share_recv.at[d - 1],
            device_id={"tile": lax.rem(me + d, n)}, device_id_type=MESH,
        )

    lax.fori_loop(1, n, spread, 0)
    keep_level = pltpu.make_async_copy(level.at[pl.ds(0, rows)], level_out, store_sem.at[0])
    keep_level.start()
    keep_dry = pltpu.make_async_copy(held.at[0], held_out.at[0], store_sem.at[4])
    keep_dry.start()

    sends = []
    keeps = [keep_dry]
    for code in (3, 2, 1):
        settle((code,))
        if code > 1:
            hop = code - 1
            send = remote(held.at[code], got_out.at[hop - 1], 6 + hop, lax.rem(me + hop, n))
            send.start()
            sends.append(send)
        keep = pltpu.make_async_copy(held.at[code], held_out.at[code], store_sem.at[code])
        keep.start()
        keeps.append(keep)

    def gather(d, _):
        share_copy(d).wait()
        return 0

    lax.fori_loop(1, n, gather, 0)
    for scenario in range(2):
        def add_share(d, value):
            return value + shares[d, scenario]

        whole = lax.fori_loop(0, n, add_share, jnp.zeros((8, 128), f32))
        energy_out[scenario] = jnp.sum(whole) / (total * half)
    keep_level.wait()
    for keep in keeps:
        keep.wait()
    for send in sends:
        send.wait()


def write_kernel(plan, level, held, got, level_out, flux_x_out, flux_y_out, resident_out):
    side = held.shape[-1]
    level_out[...] = level[...]
    for c in range(level.shape[1] // side):
        part = pl.ds(c * side, side)
        flux_x_out[:, part] = held[plan[0, c], 0].astype(jnp.float32)
        flux_y_out[:, part] = held[plan[0, c], 1].astype(jnp.float32)
    resident_out[0] = held[1].astype(jnp.float32)
    resident_out[1] = got[0].astype(jnp.float32)
    resident_out[2] = got[1].astype(jnp.float32)


def on_device(surface, flux_x, flux_y, celerity, bed_depth, roughness, smoother, block_plan):
    rows, cols = surface.shape
    side = smoother.shape[0]
    n = lax.axis_size("tile")
    f32, bf16 = jnp.float32, jnp.bfloat16
    whole = pl.BlockSpec(memory_space=pl.ANY)
    smem = pl.BlockSpec(memory_space=pltpu.SMEM)
    vmem = pl.BlockSpec(memory_space=pltpu.VMEM)
    level, held, got, energy = pl.pallas_call(
        functools.partial(window_kernel, n),
        out_shape=(
            jax.ShapeDtypeStruct((rows, cols), f32),
            jax.ShapeDtypeStruct((4, 2, side, side), bf16),
            jax.ShapeDtypeStruct((2, 2, side, side), bf16),
            jax.ShapeDtypeStruct((2,), f32),
        ),
        in_specs=[smem, vmem] + [whole] * 6,
        out_specs=(whole, whole, whole, smem),
        scratch_shapes=[
            pltpu.VMEM((rows + 8, cols), f32),
            pltpu.VMEM((rows + 8, cols), f32),
            pltpu.VMEM((rows, cols), f32),
            pltpu.VMEM((rows, cols), f32),
            pltpu.VMEM((rows, cols), f32),
            pltpu.VMEM((rows, cols), f32),
            pltpu.VMEM((3, side, side), f32),
            pltpu.VMEM((side, side), bf16),
            pltpu.VMEM((4, 2, side, side), bf16),
            pltpu.VMEM((4, 2, side, side), f32),
            pltpu.VMEM((2, 8, cols), f32),
            pltpu.VMEM((2, 8, cols), f32),
            pltpu.VMEM((2, 8, cols), f32),
            pltpu.VMEM((8, cols), f32),
            pltpu.VMEM((n, 2, 8, 128), f32),
            pltpu.SemaphoreType.DMA((6,)),
            pltpu.SemaphoreType.DMA((5,)),
            pltpu.SemaphoreType.DMA((9,)),
            pltpu.SemaphoreType.DMA((9,)),
            pltpu.SemaphoreType.DMA((n - 1,)),
            pltpu.SemaphoreType.DMA((n - 1,)),
        ],
        compiler_params=pltpu.CompilerParams(
            collective_id=0, has_side_effects=True, vmem_limit_bytes=40 * 1024 * 1024
        ),
        name="window",
    )(block_plan, smoother, surface, flux_x, flux_y, celerity, bed_depth, roughness)

    step = 64
    flat = pl.BlockSpec((step, cols), lambda i: (i, 0))
    new_surface, new_x, new_y, resident = pl.pallas_call(
        write_kernel,
        grid=(rows // step,),
        out_shape=(
            jax.ShapeDtypeStruct((rows, cols), f32),
            jax.ShapeDtypeStruct((rows, cols), f32),
            jax.ShapeDtypeStruct((rows, cols), f32),
            jax.ShapeDtypeStruct((3, 2, side, side), f32),
        ),
        in_specs=[
            smem,
            flat,
            pl.BlockSpec((4, 2, step, side), lambda i: (0, 0, i, 0)),
            pl.BlockSpec((2, 2, step, side), lambda i: (0, 0, i, 0)),
        ],
        out_specs=(flat, flat, flat, pl.BlockSpec((3, 2, step, side), lambda i: (0, 0, i, 0))),
        compiler_params=pltpu.CompilerParams(vmem_limit_bytes=20 * 1024 * 1024),
        name="write_out",
    )(block_plan, level, held, got)
    return new_surface, new_x, new_y, resident, energy


def solution(mesh):
    fields = P(("ens", "tile"), None)
    return jax.shard_map(
        on_device,
        mesh=mesh,
        in_specs=(fields,) * 6 + (P(), fields),
        out_specs=(fields, fields, fields, P(("ens", "tile"), None, None, None), P("ens")),
        check_vma=False,
    )
```

```python
import functools

import jax
import jax.numpy as jnp
from jax import lax
from jax.experimental import pallas as pl
from jax.experimental.pallas import tpu as pltpu
from jax.sharding import PartitionSpec as P

STEPS = 2
SUB = 12
STRIP = 16
MESH = pl.DeviceIdType.MESH


def window_kernel(
    n, plan_in, smoother_in, surface_in, flux_x_in, flux_y_in, celerity_in, bed_in, rough_in,
    level_out, held_out, got_out, energy_out,
    level, flux_x, flux_y, celerity, bed, rough, drag, turned, held, settled,
    below, above_level, above_flux, above_celerity, shares,
    plan, s_ref, load_sem, store_sem, send_sem, recv_sem, share_send, share_recv,
):
    rows, cols = flux_y.shape
    side = s_ref.shape[0]
    blocks = cols // side
    half = cols // 2
    me = lax.axis_index("tile")
    ahead_tile = lax.rem(me + 1, n)
    behind_tile = lax.rem(me + n - 1, n)
    top = me == 0
    bottom = me == n - 1
    f32, bf16 = jnp.float32, jnp.bfloat16

    loads = [
        pltpu.make_async_copy(source, target, load_sem.at[i])
        for i, (source, target) in enumerate(
            (
                (surface_in, level.at[pl.ds(0, rows)]),
                (celerity_in, celerity),
                (flux_x_in, flux_x.at[pl.ds(8, rows)]),
                (flux_y_in, flux_y),
                (bed_in, bed),
                (rough_in, rough),
                (smoother_in, s_ref),
                (plan_in, plan),
            )
        )
    ]
    for load in loads:
        load.start()

    barrier = pltpu.get_barrier_semaphore()

    def greet(d, _):
        pl.semaphore_signal(barrier, inc=1, device_id={"tile": lax.rem(me + d, n)}, device_id_type=MESH)
        return 0

    lax.fori_loop(1, n, greet, 0)
    pl.semaphore_wait(barrier, n - 1)

    def remote(source, target, index, device):
        return pltpu.make_async_remote_copy(
            src_ref=source, dst_ref=target, send_sem=send_sem.at[index], recv_sem=recv_sem.at[index],
            device_id={"tile": device}, device_id_type=MESH,
        )

    last = pl.ds(rows - 8, 8)
    up = [
        remote(surface_in.at[pl.ds(0, 8)], below.at[0], 0, behind_tile),
        remote(level.at[pl.ds(0, 8)], below.at[1], 1, behind_tile),
    ]
    down = [
        [
            remote(surface_in.at[last], above_level.at[0], 2, ahead_tile),
            remote(flux_x_in.at[last], above_flux.at[0], 3, ahead_tile),
            remote(celerity_in.at[last], above_celerity, 4, ahead_tile),
        ],
        [
            remote(level.at[last], above_level.at[1], 5, ahead_tile),
            remote(flux_x.at[pl.ds(rows, 8)], above_flux.at[1], 6, ahead_tile),
        ],
    ]

    @pl.when(jnp.logical_not(top))
    def _():
        up[0].start()

    @pl.when(jnp.logical_not(bottom))
    def _():
        for copy in down[0]:
            copy.start()

    for load in loads:
        load.wait()
    turned[...] = s_ref[...].astype(f32).T.astype(bf16)
    codes = [plan[0, c] for c in range(blocks)]

    def choose(options, matches):
        chosen = options[0]
        for option, match in zip(options[1:], matches[1:]):
            chosen = jnp.where(match, option, chosen)
        return chosen

    def with_code(wide, code):
        parts = [wide[:, c * side : (c + 1) * side] for c in range(blocks)]
        return choose(parts, [codes[c] == code for c in range(blocks)])

    def joined(which, at, size):
        options = [settled[code, which, pl.ds(at, size), :] for code in range(4)]
        return jnp.concatenate(
            [choose(options, [codes[c] == code for code in range(4)]) for c in range(blocks)], 1
        )

    col_ids = lax.broadcasted_iota(jnp.int32, (1, cols), 1)
    right_edge = lax.rem(col_ids, half) == half - 1
    left_edge = lax.rem(col_ids, half) == 0

    def strip_flux(step, which, at):
        if step == 0:
            return flux_x[pl.ds(8 + at, STRIP)] if which == 0 else flux_y[pl.ds(at, STRIP)]
        return joined(which, at, STRIP)

    def advance(step):
        @pl.when(bottom)
        def _():
            level[pl.ds(rows, 8)] = jnp.zeros((8, cols), f32)

        @pl.when(jnp.logical_not(bottom))
        def _():
            up[step].wait_recv()
            level[pl.ds(rows, 8)] = below[step]

        @pl.when(top)
        def _():
            flux_x[pl.ds(0, 8)] = jnp.zeros((8, cols), f32)

        @pl.when(jnp.logical_not(top))
        def _():
            for copy in down[step]:
                copy.wait_recv()
            flux_x[pl.ds(0, 8)] = above_flux[step] - above_celerity[...] * (
                level[0:1] - above_level[step]
            )

        def strip(i, _):
            at = pl.multiple_of(i * STRIP, STRIP)
            now = level[pl.ds(at, STRIP)]
            after = level[pl.ds(at + STRIP, 8)]
            ahead = pltpu.roll(jnp.concatenate([now, after], 0), STRIP + 7, 0)[:STRIP]
            wave = celerity[pl.ds(at, STRIP)]
            new_x = strip_flux(step, 0, at) - wave * (ahead - now)
            right = jnp.where(right_edge, 0.0, pltpu.roll(now, cols - 1, 1))
            new_y = strip_flux(step, 1, at) - wave * (right - now)
            behind_x = pltpu.roll(jnp.concatenate([flux_x[pl.ds(at, 8)], new_x], 0), 1, 0)[8:]
            behind_y = jnp.where(left_edge, 0.0, pltpu.roll(new_y, 1, 1))
            new_level = now - (new_x - behind_x) - (new_y - behind_y)
            flux_x[pl.ds(8 + at, STRIP)] = new_x
            level[pl.ds(at, STRIP)] = new_level
            ratio = rough[pl.ds(at, STRIP)] / jnp.maximum(new_level + bed[pl.ds(at, STRIP)], 1.0)
            ratio = ratio.astype(bf16).astype(f32)
            for code in range(1, 4):
                drag[0, code - 1, pl.ds(at, STRIP), :] = with_code(ratio, code)
            for which, new in enumerate((new_x, new_y)):
                for code in range(4):
                    mine = with_code(new, code)
                    held[code, which, pl.ds(at, STRIP), :] = mine.astype(bf16)
                    if code == 0:
                        settled[0, which, pl.ds(at, STRIP), :] = mine
            return 0

        lax.fori_loop(0, rows // STRIP, strip, 0)

    def settle(wanted):
        def product(pieces):
            tall = jnp.dot(
                jnp.concatenate(pieces, 0), turned[...], preferred_element_type=f32
            )
            return [tall[i * side : (i + 1) * side] for i in range(len(pieces))]

        def once(flip):
            pieces = [held[code, which] for code in wanted for which in range(2)]
            mixed = [piece.astype(bf16).T for piece in product(pieces)]
            smoothed = product(mixed)
            out = []
            for i, value in enumerate(smoothed):
                weight = drag[flip, wanted[i // 2] - 1]
                out.append(value * pl.reciprocal(1.0 + weight * jnp.abs(value), approx=True))
            return out

        def keep_bf16(values):
            for i, value in enumerate(values):
                held[wanted[i // 2], i % 2] = value.astype(bf16)

        for code in wanted:
            drag[1, code - 1] = drag[0, code - 1].T

        def body(i, _):
            keep_bf16(once(1))
            keep_bf16(once(0))
            return 0

        lax.fori_loop(0, SUB // 2 - 1, body, 0)
        keep_bf16(once(1))
        values = once(0)
        keep_bf16(values)
        for i, value in enumerate(values):
            settled[wanted[i // 2], i % 2] = value

    advance(0)
    for copy, edge in ((up[0], top), (down[0][0], bottom), (down[0][1], bottom), (down[0][2], bottom)):
        @pl.when(jnp.logical_not(edge))
        def _():
            copy.wait_send()

    @pl.when(jnp.logical_not(top))
    def _():
        up[1].start()

    @pl.when(jnp.logical_not(bottom))
    def _():
        down[1][0].start()

    settle((1, 2, 3))
    flux_x[pl.ds(rows, 8)] = joined(0, rows - 8, 8)

    @pl.when(jnp.logical_not(top))
    def _():
        up[1].wait_send()

    @pl.when(jnp.logical_not(bottom))
    def _():
        down[1][1].start()
        down[1][0].wait_send()
        down[1][1].wait_send()

    advance(1)

    total = n * rows

    def add_up(i, sums):
        at = pl.multiple_of(i * 8, 8)
        row = (me * rows + at + lax.broadcasted_iota(jnp.int32, (8, 1), 0)).astype(f32)
        value = level[pl.ds(at, 8)]
        return sums + (1.0 + 2.0 * row / total) * (value * value)

    sums = lax.fori_loop(0, rows // 8, add_up, jnp.zeros((8, cols), f32))
    for scenario in range(2):
        share = jnp.zeros((8, 128), f32)
        for c in range(half // 128):
            share = share + sums[:, scenario * half + c * 128 : scenario * half + (c + 1) * 128]
        shares[me, scenario] = share

    def spread(d, _):
        share_copy(d).start()
        return 0

    def share_copy(d):
        return pltpu.make_async_remote_copy(
            src_ref=shares.at[me], dst_ref=shares.at[me],
            send_sem=share_send.at[d - 1], recv_sem=share_recv.at[d - 1],
            device_id={"tile": lax.rem(me + d, n)}, device_id_type=MESH,
        )

    lax.fori_loop(1, n, spread, 0)
    keep_level = pltpu.make_async_copy(level.at[pl.ds(0, rows)], level_out, store_sem.at[0])
    keep_level.start()
    keep_dry = pltpu.make_async_copy(held.at[0], held_out.at[0], store_sem.at[4])
    keep_dry.start()

    sends = []
    keeps = [keep_dry]
    for code in (3, 2, 1):
        settle((code,))
        if code > 1:
            hop = code - 1
            send = remote(held.at[code], got_out.at[hop - 1], 6 + hop, lax.rem(me + hop, n))
            send.start()
            sends.append(send)
        keep = pltpu.make_async_copy(held.at[code], held_out.at[code], store_sem.at[code])
        keep.start()
        keeps.append(keep)

    def gather(d, _):
        share_copy(d).wait()
        return 0

    lax.fori_loop(1, n, gather, 0)
    for scenario in range(2):
        def add_share(d, value):
            return value + shares[d, scenario]

        whole = lax.fori_loop(0, n, add_share, jnp.zeros((8, 128), f32))
        energy_out[scenario] = jnp.sum(whole) / (total * half)
    keep_level.wait()
    for keep in keeps:
        keep.wait()
    for send in sends:
        send.wait()


def write_kernel(plan, level, held, got, level_out, flux_x_out, flux_y_out, resident_out):
    side = held.shape[-1]
    level_out[...] = level[...]
    for c in range(level.shape[1] // side):
        part = pl.ds(c * side, side)
        flux_x_out[:, part] = held[plan[0, c], 0].astype(jnp.float32)
        flux_y_out[:, part] = held[plan[0, c], 1].astype(jnp.float32)
    resident_out[0] = held[1].astype(jnp.float32)
    resident_out[1] = got[0].astype(jnp.float32)
    resident_out[2] = got[1].astype(jnp.float32)


def on_device(surface, flux_x, flux_y, celerity, bed_depth, roughness, smoother, block_plan):
    rows, cols = surface.shape
    side = smoother.shape[0]
    n = lax.axis_size("tile")
    f32, bf16 = jnp.float32, jnp.bfloat16
    whole = pl.BlockSpec(memory_space=pltpu.HBM)
    smem = pl.BlockSpec(memory_space=pltpu.SMEM)
    level, held, got, energy = pl.pallas_call(
        functools.partial(window_kernel, n),
        out_shape=(
            jax.ShapeDtypeStruct((rows, cols), f32),
            jax.ShapeDtypeStruct((4, 2, side, side), bf16),
            jax.ShapeDtypeStruct((2, 2, side, side), bf16),
            jax.ShapeDtypeStruct((2,), f32),
        ),
        in_specs=[whole] * 8,
        out_specs=(whole, whole, whole, smem),
        scratch_shapes=[
            pltpu.VMEM((rows + 8, cols), f32),
            pltpu.VMEM((rows + 8, cols), f32),
            pltpu.VMEM((rows, cols), f32),
            pltpu.VMEM((rows, cols), f32),
            pltpu.VMEM((rows, cols), f32),
            pltpu.VMEM((rows, cols), f32),
            pltpu.VMEM((2, 3, side, side), f32),
            pltpu.VMEM((side, side), bf16),
            pltpu.VMEM((4, 2, side, side), bf16),
            pltpu.VMEM((4, 2, side, side), f32),
            pltpu.VMEM((2, 8, cols), f32),
            pltpu.VMEM((2, 8, cols), f32),
            pltpu.VMEM((2, 8, cols), f32),
            pltpu.VMEM((8, cols), f32),
            pltpu.VMEM((n, 2, 8, 128), f32),
            pltpu.SMEM(block_plan.shape, jnp.int32),
            pltpu.VMEM((side, side), bf16),
            pltpu.SemaphoreType.DMA((8,)),
            pltpu.SemaphoreType.DMA((5,)),
            pltpu.SemaphoreType.DMA((9,)),
            pltpu.SemaphoreType.DMA((9,)),
            pltpu.SemaphoreType.DMA((n - 1,)),
            pltpu.SemaphoreType.DMA((n - 1,)),
        ],
        compiler_params=pltpu.CompilerParams(
            collective_id=0, has_side_effects=True, vmem_limit_bytes=56 * 1024 * 1024
        ),
        name="window",
    )(block_plan, smoother, surface, flux_x, flux_y, celerity, bed_depth, roughness)

    step = 64
    flat = pl.BlockSpec((step, cols), lambda i: (i, 0))
    new_surface, new_x, new_y, resident = pl.pallas_call(
        write_kernel,
        grid=(rows // step,),
        out_shape=(
            jax.ShapeDtypeStruct((rows, cols), f32),
            jax.ShapeDtypeStruct((rows, cols), f32),
            jax.ShapeDtypeStruct((rows, cols), f32),
            jax.ShapeDtypeStruct((3, 2, side, side), f32),
        ),
        in_specs=[
            smem,
            flat,
            pl.BlockSpec((4, 2, step, side), lambda i: (0, 0, i, 0)),
            pl.BlockSpec((2, 2, step, side), lambda i: (0, 0, i, 0)),
        ],
        out_specs=(flat, flat, flat, pl.BlockSpec((3, 2, step, side), lambda i: (0, 0, i, 0))),
        compiler_params=pltpu.CompilerParams(vmem_limit_bytes=20 * 1024 * 1024),
        name="write_out",
    )(block_plan, level, held, got)
    return new_surface, new_x, new_y, resident, energy


def solution(mesh):
    fields = P(("ens", "tile"), None)
    return jax.shard_map(
        on_device,
        mesh=mesh,
        in_specs=(fields,) * 6 + (P(), fields),
        out_specs=(fields, fields, fields, P(("ens", "tile"), None, None, None), P("ens")),
        check_vma=False,
    )
```

```python
import functools

import jax
import jax.numpy as jnp
from jax import lax
from jax.experimental import pallas as pl
from jax.experimental.pallas import tpu as pltpu
from jax.sharding import PartitionSpec as P

STEPS = 2
SUB = 12
STRIP = 16
MESH = pl.DeviceIdType.MESH


def window_kernel(
    n, plan_in, smoother_in, surface_in, flux_x_in, flux_y_in, celerity_in, bed_in, rough_in,
    level_out, held_out, got_out, energy_out,
    level, flux_x, flux_y, celerity, bed, rough, drag, turned, held, settled,
    below, above_level, above_flux, above_celerity, shares,
    plan, s_ref, load_sem, store_sem, send_sem, recv_sem, share_send, share_recv,
):
    rows, cols = flux_y.shape
    side = s_ref.shape[0]
    blocks = cols // side
    half = cols // 2
    me = lax.axis_index("tile")
    ahead_tile = lax.rem(me + 1, n)
    behind_tile = lax.rem(me + n - 1, n)
    top = me == 0
    bottom = me == n - 1
    f32, bf16 = jnp.float32, jnp.bfloat16

    loads = [
        pltpu.make_async_copy(source, target, load_sem.at[i])
        for i, (source, target) in enumerate(
            (
                (surface_in, level.at[pl.ds(0, rows)]),
                (celerity_in, celerity),
                (flux_x_in, flux_x.at[pl.ds(8, rows)]),
                (flux_y_in, flux_y),
                (bed_in, bed),
                (rough_in, rough),
                (smoother_in, s_ref),
                (plan_in, plan),
            )
        )
    ]
    for load in loads:
        load.start()

    barrier = pltpu.get_barrier_semaphore()

    def greet(d, _):
        pl.semaphore_signal(barrier, inc=1, device_id={"tile": lax.rem(me + d, n)}, device_id_type=MESH)
        return 0

    lax.fori_loop(1, n, greet, 0)
    pl.semaphore_wait(barrier, n - 1)

    def remote(source, target, index, device):
        return pltpu.make_async_remote_copy(
            src_ref=source, dst_ref=target, send_sem=send_sem.at[index], recv_sem=recv_sem.at[index],
            device_id={"tile": device}, device_id_type=MESH,
        )

    last = pl.ds(rows - 8, 8)
    up = [
        remote(surface_in.at[pl.ds(0, 8)], below.at[0], 0, behind_tile),
        remote(level.at[pl.ds(0, 8)], below.at[1], 1, behind_tile),
    ]
    down = [
        [
            remote(surface_in.at[last], above_level.at[0], 2, ahead_tile),
            remote(flux_x_in.at[last], above_flux.at[0], 3, ahead_tile),
            remote(celerity_in.at[last], above_celerity, 4, ahead_tile),
        ],
        [
            remote(level.at[last], above_level.at[1], 5, ahead_tile),
            remote(flux_x.at[pl.ds(rows, 8)], above_flux.at[1], 6, ahead_tile),
        ],
    ]

    @pl.when(jnp.logical_not(top))
    def _():
        up[0].start()

    @pl.when(jnp.logical_not(bottom))
    def _():
        for copy in down[0]:
            copy.start()

    for load in loads:
        load.wait()
    turned[...] = s_ref[...].astype(f32).T.astype(bf16)
    codes = [plan[0, c] for c in range(blocks)]

    def choose(options, matches):
        chosen = options[0]
        for option, match in zip(options[1:], matches[1:]):
            chosen = jnp.where(match, option, chosen)
        return chosen

    def with_code(wide, code):
        parts = [wide[:, c * side : (c + 1) * side] for c in range(blocks)]
        return choose(parts, [codes[c] == code for c in range(blocks)])

    def joined(which, at, size):
        options = [settled[code, which, pl.ds(at, size), :] for code in range(4)]
        return jnp.concatenate(
            [choose(options, [codes[c] == code for code in range(4)]) for c in range(blocks)], 1
        )

    col_ids = lax.broadcasted_iota(jnp.int32, (1, cols), 1)
    right_edge = lax.rem(col_ids, half) == half - 1
    left_edge = lax.rem(col_ids, half) == 0

    def strip_flux(step, which, at):
        if step == 0:
            return flux_x[pl.ds(8 + at, STRIP)] if which == 0 else flux_y[pl.ds(at, STRIP)]
        return joined(which, at, STRIP)

    def advance(step):
        @pl.when(bottom)
        def _():
            level[pl.ds(rows, 8)] = jnp.zeros((8, cols), f32)

        @pl.when(jnp.logical_not(bottom))
        def _():
            up[step].wait_recv()
            level[pl.ds(rows, 8)] = below[step]

        @pl.when(top)
        def _():
            flux_x[pl.ds(0, 8)] = jnp.zeros((8, cols), f32)

        @pl.when(jnp.logical_not(top))
        def _():
            for copy in down[step]:
                copy.wait_recv()
            flux_x[pl.ds(0, 8)] = above_flux[step] - above_celerity[...] * (
                level[0:1] - above_level[step]
            )

        def strip(i, _):
            at = pl.multiple_of(i * STRIP, STRIP)
            now = level[pl.ds(at, STRIP)]
            after = level[pl.ds(at + STRIP, 8)]
            ahead = pltpu.roll(jnp.concatenate([now, after], 0), STRIP + 7, 0)[:STRIP]
            wave = celerity[pl.ds(at, STRIP)]
            new_x = strip_flux(step, 0, at) - wave * (ahead - now)
            right = jnp.where(right_edge, 0.0, pltpu.roll(now, cols - 1, 1))
            new_y = strip_flux(step, 1, at) - wave * (right - now)
            behind_x = pltpu.roll(jnp.concatenate([flux_x[pl.ds(at, 8)], new_x], 0), 1, 0)[8:]
            behind_y = jnp.where(left_edge, 0.0, pltpu.roll(new_y, 1, 1))
            new_level = now - (new_x - behind_x) - (new_y - behind_y)
            flux_x[pl.ds(8 + at, STRIP)] = new_x
            level[pl.ds(at, STRIP)] = new_level
            ratio = rough[pl.ds(at, STRIP)] / jnp.maximum(new_level + bed[pl.ds(at, STRIP)], 1.0)
            ratio = ratio.astype(bf16).astype(f32)
            for code in range(1, 4):
                drag[0, code - 1, pl.ds(at, STRIP), :] = with_code(ratio, code)
            for which, new in enumerate((new_x, new_y)):
                for code in range(4):
                    mine = with_code(new, code)
                    held[code, which, pl.ds(at, STRIP), :] = mine.astype(bf16)
                    if code == 0:
                        settled[0, which, pl.ds(at, STRIP), :] = mine
            return 0

        lax.fori_loop(0, rows // STRIP, strip, 0)

    def settle(wanted):
        def product(pieces):
            tall = jnp.dot(
                jnp.concatenate(pieces, 0), turned[...], preferred_element_type=f32
            )
            return [tall[i * side : (i + 1) * side] for i in range(len(pieces))]

        def once(flip):
            pieces = [held[code, which] for code, which in wanted]
            mixed = [piece.astype(bf16).T for piece in product(pieces)]
            smoothed = product(mixed)
            out = []
            for i, value in enumerate(smoothed):
                weight = drag[flip, wanted[i][0] - 1]
                out.append(value * pl.reciprocal(1.0 + weight * jnp.abs(value), approx=True))
            return out

        def keep_bf16(values):
            for i, value in enumerate(values):
                held[wanted[i]] = value.astype(bf16)

        for code in sorted({code for code, _ in wanted}):
            drag[1, code - 1] = drag[0, code - 1].T

        def body(i, _):
            keep_bf16(once(1))
            keep_bf16(once(0))
            return 0

        lax.fori_loop(0, SUB // 2 - 1, body, 0)
        keep_bf16(once(1))
        values = once(0)
        keep_bf16(values)
        for i, value in enumerate(values):
            settled[wanted[i]] = value

    advance(0)
    for copy, edge in ((up[0], top), (down[0][0], bottom), (down[0][1], bottom), (down[0][2], bottom)):
        @pl.when(jnp.logical_not(edge))
        def _():
            copy.wait_send()

    @pl.when(jnp.logical_not(top))
    def _():
        up[1].start()

    @pl.when(jnp.logical_not(bottom))
    def _():
        down[1][0].start()

    settle([(code, which) for code in (1, 2, 3) for which in range(2)])
    flux_x[pl.ds(rows, 8)] = joined(0, rows - 8, 8)

    @pl.when(jnp.logical_not(top))
    def _():
        up[1].wait_send()

    @pl.when(jnp.logical_not(bottom))
    def _():
        down[1][1].start()
        down[1][0].wait_send()
        down[1][1].wait_send()

    advance(1)

    total = n * rows

    def add_up(i, sums):
        at = pl.multiple_of(i * 8, 8)
        row = (me * rows + at + lax.broadcasted_iota(jnp.int32, (8, 1), 0)).astype(f32)
        value = level[pl.ds(at, 8)]
        return sums + (1.0 + 2.0 * row / total) * (value * value)

    sums = lax.fori_loop(0, rows // 8, add_up, jnp.zeros((8, cols), f32))
    for scenario in range(2):
        share = jnp.zeros((8, 128), f32)
        for c in range(half // 128):
            share = share + sums[:, scenario * half + c * 128 : scenario * half + (c + 1) * 128]
        shares[me, scenario] = share

    def spread(d, _):
        share_copy(d).start()
        return 0

    def share_copy(d):
        return pltpu.make_async_remote_copy(
            src_ref=shares.at[me], dst_ref=shares.at[me],
            send_sem=share_send.at[d - 1], recv_sem=share_recv.at[d - 1],
            device_id={"tile": lax.rem(me + d, n)}, device_id_type=MESH,
        )

    lax.fori_loop(1, n, spread, 0)
    keep_level = pltpu.make_async_copy(level.at[pl.ds(0, rows)], level_out, store_sem.at[0])
    keep_level.start()
    keep_dry = pltpu.make_async_copy(held.at[0], held_out.at[0], store_sem.at[4])
    keep_dry.start()

    sends = []
    keeps = [keep_dry]
    for code in (3, 2):
        settle([(code, 0), (code, 1), (1, 3 - code)])
        hop = code - 1
        send = remote(held.at[code], got_out.at[hop - 1], 6 + hop, lax.rem(me + hop, n))
        send.start()
        sends.append(send)
        keep = pltpu.make_async_copy(held.at[code], held_out.at[code], store_sem.at[code])
        keep.start()
        keeps.append(keep)
    keep = pltpu.make_async_copy(held.at[1], held_out.at[1], store_sem.at[1])
    keep.start()
    keeps.append(keep)

    def gather(d, _):
        share_copy(d).wait()
        return 0

    lax.fori_loop(1, n, gather, 0)
    for scenario in range(2):
        def add_share(d, value):
            return value + shares[d, scenario]

        whole = lax.fori_loop(0, n, add_share, jnp.zeros((8, 128), f32))
        energy_out[scenario] = jnp.sum(whole) / (total * half)
    keep_level.wait()
    for keep in keeps:
        keep.wait()
    for send in sends:
        send.wait()


def write_kernel(plan, level, held, got, level_out, flux_x_out, flux_y_out, resident_out):
    side = held.shape[-1]
    level_out[...] = level[...]
    for c in range(level.shape[1] // side):
        part = pl.ds(c * side, side)
        flux_x_out[:, part] = held[plan[0, c], 0].astype(jnp.float32)
        flux_y_out[:, part] = held[plan[0, c], 1].astype(jnp.float32)
    resident_out[0] = held[1].astype(jnp.float32)
    resident_out[1] = got[0].astype(jnp.float32)
    resident_out[2] = got[1].astype(jnp.float32)


def on_device(surface, flux_x, flux_y, celerity, bed_depth, roughness, smoother, block_plan):
    rows, cols = surface.shape
    side = smoother.shape[0]
    n = lax.axis_size("tile")
    f32, bf16 = jnp.float32, jnp.bfloat16
    whole = pl.BlockSpec(memory_space=pltpu.HBM)
    smem = pl.BlockSpec(memory_space=pltpu.SMEM)
    level, held, got, energy = pl.pallas_call(
        functools.partial(window_kernel, n),
        out_shape=(
            jax.ShapeDtypeStruct((rows, cols), f32),
            jax.ShapeDtypeStruct((4, 2, side, side), bf16),
            jax.ShapeDtypeStruct((2, 2, side, side), bf16),
            jax.ShapeDtypeStruct((2,), f32),
        ),
        in_specs=[whole] * 8,
        out_specs=(whole, whole, whole, smem),
        scratch_shapes=[
            pltpu.VMEM((rows + 8, cols), f32),
            pltpu.VMEM((rows + 8, cols), f32),
            pltpu.VMEM((rows, cols), f32),
            pltpu.VMEM((rows, cols), f32),
            pltpu.VMEM((rows, cols), f32),
            pltpu.VMEM((rows, cols), f32),
            pltpu.VMEM((2, 3, side, side), f32),
            pltpu.VMEM((side, side), bf16),
            pltpu.VMEM((4, 2, side, side), bf16),
            pltpu.VMEM((4, 2, side, side), f32),
            pltpu.VMEM((2, 8, cols), f32),
            pltpu.VMEM((2, 8, cols), f32),
            pltpu.VMEM((2, 8, cols), f32),
            pltpu.VMEM((8, cols), f32),
            pltpu.VMEM((n, 2, 8, 128), f32),
            pltpu.SMEM(block_plan.shape, jnp.int32),
            pltpu.VMEM((side, side), bf16),
            pltpu.SemaphoreType.DMA((8,)),
            pltpu.SemaphoreType.DMA((5,)),
            pltpu.SemaphoreType.DMA((9,)),
            pltpu.SemaphoreType.DMA((9,)),
            pltpu.SemaphoreType.DMA((n - 1,)),
            pltpu.SemaphoreType.DMA((n - 1,)),
        ],
        compiler_params=pltpu.CompilerParams(
            collective_id=0, has_side_effects=True, vmem_limit_bytes=56 * 1024 * 1024
        ),
        name="window",
    )(block_plan, smoother, surface, flux_x, flux_y, celerity, bed_depth, roughness)

    step = 64
    flat = pl.BlockSpec((step, cols), lambda i: (i, 0))
    new_surface, new_x, new_y, resident = pl.pallas_call(
        write_kernel,
        grid=(rows // step,),
        out_shape=(
            jax.ShapeDtypeStruct((rows, cols), f32),
            jax.ShapeDtypeStruct((rows, cols), f32),
            jax.ShapeDtypeStruct((rows, cols), f32),
            jax.ShapeDtypeStruct((3, 2, side, side), f32),
        ),
        in_specs=[
            smem,
            flat,
            pl.BlockSpec((4, 2, step, side), lambda i: (0, 0, i, 0)),
            pl.BlockSpec((2, 2, step, side), lambda i: (0, 0, i, 0)),
        ],
        out_specs=(flat, flat, flat, pl.BlockSpec((3, 2, step, side), lambda i: (0, 0, i, 0))),
        compiler_params=pltpu.CompilerParams(vmem_limit_bytes=56 * 1024 * 1024),
        name="write_out",
    )(block_plan, level, held, got)
    return new_surface, new_x, new_y, resident, energy


def solution(mesh):
    fields = P(("ens", "tile"), None)
    return jax.shard_map(
        on_device,
        mesh=mesh,
        in_specs=(fields,) * 6 + (P(), fields),
        out_specs=(fields, fields, fields, P(("ens", "tile"), None, None, None), P("ens")),
        check_vma=False,
    )
```

```python
import functools

import jax
import jax.numpy as jnp
from jax import lax
from jax.experimental import pallas as pl
from jax.experimental.pallas import tpu as pltpu
from jax.sharding import PartitionSpec as P

STEPS = 2
SUB = 12
STRIP = 16
MESH = pl.DeviceIdType.MESH


def window_kernel(
    n, plan_in, smoother_in, surface_in, flux_x_in, flux_y_in, celerity_in, bed_in, rough_in,
    level_out, held_out, got_out, energy_out,
    level, flux_x, flux_y, celerity, bed, rough, drag, turned, held, settled,
    below, above_level, above_flux, above_celerity, rim, shares,
    plan, s_ref, load_sem, store_sem, send_sem, recv_sem, share_send, share_recv,
):
    rows, cols = flux_y.shape
    side = s_ref.shape[0]
    blocks = cols // side
    half = cols // 2
    me = lax.axis_index("tile")
    ahead_tile = lax.rem(me + 1, n)
    behind_tile = lax.rem(me + n - 1, n)
    top = me == 0
    bottom = me == n - 1
    f32, bf16 = jnp.float32, jnp.bfloat16

    cut = rows // 2
    sources = (
        (surface_in, level, 0),
        (celerity_in, celerity, 0),
        (flux_x_in, flux_x, 8),
        (flux_y_in, flux_y, 0),
        (bed_in, bed, 0),
        (rough_in, rough, 0),
    )
    loads = [
        [
            pltpu.make_async_copy(
                source.at[pl.ds(part * cut, cut)], target.at[pl.ds(lead + part * cut, cut)], load_sem.at[part, i]
            )
            for i, (source, target, lead) in enumerate(sources)
        ]
        for part in range(2)
    ]
    loads[0] += [
        pltpu.make_async_copy(smoother_in, s_ref, load_sem.at[0, 6]),
        pltpu.make_async_copy(plan_in, plan, load_sem.at[0, 7]),
    ]
    for part in range(2):
        for load in loads[part]:
            load.start()

    barrier = pltpu.get_barrier_semaphore()

    def greet(d, _):
        pl.semaphore_signal(barrier, inc=1, device_id={"tile": lax.rem(me + d, n)}, device_id_type=MESH)
        return 0

    lax.fori_loop(1, n, greet, 0)
    pl.semaphore_wait(barrier, n - 1)

    def remote(source, target, index, device):
        return pltpu.make_async_remote_copy(
            src_ref=source, dst_ref=target, send_sem=send_sem.at[index], recv_sem=recv_sem.at[index],
            device_id={"tile": device}, device_id_type=MESH,
        )

    last = pl.ds(rows - 8, 8)
    up = [
        remote(surface_in.at[pl.ds(0, 8)], below.at[0], 0, behind_tile),
        remote(level.at[pl.ds(0, 8)], below.at[1], 1, behind_tile),
    ]
    down = [
        [
            remote(surface_in.at[last], above_level.at[0], 2, ahead_tile),
            remote(flux_x_in.at[last], above_flux.at[0], 3, ahead_tile),
            remote(celerity_in.at[last], above_celerity, 4, ahead_tile),
        ],
        [
            remote(level.at[last], above_level.at[1], 5, ahead_tile),
            remote(rim, above_flux.at[1], 6, ahead_tile),
        ],
    ]

    @pl.when(jnp.logical_not(top))
    def _():
        up[0].start()

    @pl.when(jnp.logical_not(bottom))
    def _():
        for copy in down[0]:
            copy.start()

    for load in loads[0]:
        load.wait()
    turned[...] = s_ref[...].astype(f32).T.astype(bf16)
    codes = [plan[0, c] for c in range(blocks)]

    def choose(options, matches):
        chosen = options[0]
        for option, match in zip(options[1:], matches[1:]):
            chosen = jnp.where(match, option, chosen)
        return chosen

    def with_code(wide, code):
        parts = [wide[:, c * side : (c + 1) * side] for c in range(blocks)]
        return choose(parts, [codes[c] == code for c in range(blocks)])

    def joined(which, at, size):
        options = [settled[code, which, pl.ds(at, size), :] for code in range(4)]
        return jnp.concatenate(
            [choose(options, [codes[c] == code for code in range(4)]) for c in range(blocks)], 1
        )

    col_ids = lax.broadcasted_iota(jnp.int32, (1, cols), 1)
    right_edge = lax.rem(col_ids, half) == half - 1
    left_edge = lax.rem(col_ids, half) == 0

    def strip_flux(step, which, at):
        if step == 0:
            return flux_x[pl.ds(8 + at, STRIP)] if which == 0 else flux_y[pl.ds(at, STRIP)]
        return joined(which, at, STRIP)

    def drag_of(at, new_level):
        ratio = rough[pl.ds(at, STRIP)] / jnp.maximum(new_level + bed[pl.ds(at, STRIP)], 1.0)
        ratio = ratio.astype(bf16)
        for code in range(1, 4):
            drag[0, code - 1, pl.ds(at, STRIP), :] = with_code(ratio, code)

    def advance(step):
        flux_x[pl.ds(0, 8)] = jnp.zeros((8, cols), f32)
        old_first = level[0:1]

        def strip(i, _):
            at = pl.multiple_of(i * STRIP, STRIP)
            now = level[pl.ds(at, STRIP)]
            after = level[pl.ds(at + STRIP, 8)]
            ahead = pltpu.roll(jnp.concatenate([now, after], 0), STRIP + 7, 0)[:STRIP]
            wave = celerity[pl.ds(at, STRIP)]
            new_x = strip_flux(step, 0, at) - wave * (ahead - now)
            right = jnp.where(right_edge, 0.0, pltpu.roll(now, cols - 1, 1))
            new_y = strip_flux(step, 1, at) - wave * (right - now)
            behind_x = pltpu.roll(jnp.concatenate([flux_x[pl.ds(at, 8)], new_x], 0), 1, 0)[8:]
            behind_y = jnp.where(left_edge, 0.0, pltpu.roll(new_y, 1, 1))
            new_level = now - (new_x - behind_x) - (new_y - behind_y)
            flux_x[pl.ds(8 + at, STRIP)] = new_x
            level[pl.ds(at, STRIP)] = new_level
            drag_of(at, new_level)
            for which, new in enumerate((new_x, new_y)):
                for code in range(4):
                    mine = with_code(new, code)
                    held[code, which, pl.ds(at, STRIP), :] = mine.astype(bf16)
                    if code == 0:
                        settled[0, which, pl.ds(at, STRIP), :] = mine
            return 0

        count = rows // STRIP
        if step == 0:
            lax.fori_loop(0, count // 2 - 1, strip, 0)
            for load in loads[1]:
                load.wait()
            lax.fori_loop(count // 2 - 1, count - 1, strip, 0, unroll=2)
        else:
            lax.fori_loop(0, count - 1, strip, 0, unroll=3)

        @pl.when(bottom)
        def _():
            level[pl.ds(rows, 8)] = jnp.zeros((8, cols), f32)

        @pl.when(jnp.logical_not(bottom))
        def _():
            up[step].wait_recv()
            level[pl.ds(rows, 8)] = below[step]

        strip(count - 1, 0)

        @pl.when(jnp.logical_not(top))
        def _():
            for copy in down[step]:
                copy.wait_recv()
            above = above_flux[step] - above_celerity[...] * (old_first - above_level[step])
            first = lax.broadcasted_iota(jnp.int32, (8, 1), 0) == 0
            level[pl.ds(0, 8)] = level[pl.ds(0, 8)] + jnp.where(first, pltpu.roll(above, 1, 0), 0.0)
            drag_of(0, level[pl.ds(0, STRIP)])

    def settle(wanted):
        def product(pieces):
            tall = jnp.dot(
                jnp.concatenate(pieces, 0), turned[...], preferred_element_type=f32
            )
            return [tall[i * side : (i + 1) * side] for i in range(len(pieces))]

        def raw(flip):
            pieces = [held[code, which] for code, which in wanted]
            mixed = [piece.astype(bf16).T for piece in product(pieces)]
            return product(mixed)

        def repeat(flip):
            for i, value in enumerate(raw(flip)):
                weight = drag[flip, wanted[i][0] - 1]
                value = value.astype(bf16)
                held[wanted[i]] = value * pl.reciprocal(1 + weight * jnp.abs(value), approx=True)

        for code in sorted({code for code, _ in wanted}):
            drag[1, code - 1] = drag[0, code - 1].T

        def body(i, _):
            repeat(1)
            repeat(0)
            return 0

        lax.fori_loop(0, SUB // 2 - 1, body, 0)
        repeat(1)
        for i, value in enumerate(raw(0)):
            weight = drag[0, wanted[i][0] - 1].astype(f32)
            value = value / (1.0 + weight * jnp.abs(value))
            settled[wanted[i]] = value
            held[wanted[i]] = value.astype(bf16)

    advance(0)
    for copy, edge in ((up[0], top), (down[0][0], bottom), (down[0][1], bottom), (down[0][2], bottom)):
        @pl.when(jnp.logical_not(edge))
        def _():
            copy.wait_send()

    @pl.when(jnp.logical_not(top))
    def _():
        up[1].start()

    @pl.when(jnp.logical_not(bottom))
    def _():
        down[1][0].start()

    settle([(code, which) for code in (1, 2, 3) for which in range(2)])
    rim[...] = joined(0, rows - 8, 8)

    @pl.when(jnp.logical_not(top))
    def _():
        up[1].wait_send()

    @pl.when(jnp.logical_not(bottom))
    def _():
        down[1][1].start()
        down[1][0].wait_send()

    advance(1)

    total = n * rows

    def add_up(i, sums):
        at = pl.multiple_of(i * 8, 8)
        row = (me * rows + at + lax.broadcasted_iota(jnp.int32, (8, 1), 0)).astype(f32)
        value = level[pl.ds(at, 8)]
        return sums + (1.0 + 2.0 * row / total) * (value * value)

    sums = lax.fori_loop(0, rows // 8, add_up, jnp.zeros((8, cols), f32), unroll=4)
    for scenario in range(2):
        share = jnp.zeros((8, 128), f32)
        for c in range(half // 128):
            share = share + sums[:, scenario * half + c * 128 : scenario * half + (c + 1) * 128]
        shares[me, scenario] = share

    def spread(d, _):
        share_copy(d).start()
        return 0

    def share_copy(d):
        return pltpu.make_async_remote_copy(
            src_ref=shares.at[me], dst_ref=shares.at[me],
            send_sem=share_send.at[d - 1], recv_sem=share_recv.at[d - 1],
            device_id={"tile": lax.rem(me + d, n)}, device_id_type=MESH,
        )

    lax.fori_loop(1, n, spread, 0)
    keep_level = pltpu.make_async_copy(level.at[pl.ds(0, rows)], level_out, store_sem.at[0])
    keep_level.start()
    keep_dry = pltpu.make_async_copy(held.at[0], held_out.at[0], store_sem.at[4])
    keep_dry.start()

    sends = []
    keeps = [keep_dry]
    for code in (3, 2):
        settle([(code, 0), (code, 1), (1, 3 - code)])
        hop = code - 1
        send = remote(held.at[code], got_out.at[hop - 1], 6 + hop, lax.rem(me + hop, n))
        send.start()
        sends.append(send)
        keep = pltpu.make_async_copy(held.at[code], held_out.at[code], store_sem.at[code])
        keep.start()
        keeps.append(keep)
    keep = pltpu.make_async_copy(held.at[1], held_out.at[1], store_sem.at[1])
    keep.start()
    keeps.append(keep)

    def gather(d, _):
        share_copy(d).wait()
        return 0

    lax.fori_loop(1, n, gather, 0)
    for scenario in range(2):
        def add_share(d, value):
            return value + shares[d, scenario]

        whole = lax.fori_loop(0, n, add_share, jnp.zeros((8, 128), f32))
        energy_out[scenario] = jnp.sum(whole) / (total * half)
    keep_level.wait()
    for keep in keeps:
        keep.wait()
    for send in sends:
        send.wait()

    @pl.when(jnp.logical_not(bottom))
    def _():
        down[1][1].wait_send()


def write_kernel(plan, level, held, got, level_out, flux_x_out, flux_y_out, resident_out):
    side = held.shape[-1]
    level_out[...] = level[...]
    for c in range(level.shape[1] // side):
        part = pl.ds(c * side, side)
        flux_x_out[:, part] = held[plan[0, c], 0].astype(jnp.float32)
        flux_y_out[:, part] = held[plan[0, c], 1].astype(jnp.float32)
    resident_out[0] = held[1].astype(jnp.float32)
    resident_out[1] = got[0].astype(jnp.float32)
    resident_out[2] = got[1].astype(jnp.float32)


def on_device(surface, flux_x, flux_y, celerity, bed_depth, roughness, smoother, block_plan):
    rows, cols = surface.shape
    side = smoother.shape[0]
    n = lax.axis_size("tile")
    f32, bf16 = jnp.float32, jnp.bfloat16
    whole = pl.BlockSpec(memory_space=pltpu.HBM)
    smem = pl.BlockSpec(memory_space=pltpu.SMEM)
    level, held, got, energy = pl.pallas_call(
        functools.partial(window_kernel, n),
        out_shape=(
            jax.ShapeDtypeStruct((rows, cols), f32),
            jax.ShapeDtypeStruct((4, 2, side, side), bf16),
            jax.ShapeDtypeStruct((2, 2, side, side), bf16),
            jax.ShapeDtypeStruct((2,), f32),
        ),
        in_specs=[whole] * 8,
        out_specs=(whole, whole, whole, smem),
        scratch_shapes=[
            pltpu.VMEM((rows + 8, cols), f32),
            pltpu.VMEM((rows + 8, cols), f32),
            pltpu.VMEM((rows, cols), f32),
            pltpu.VMEM((rows, cols), f32),
            pltpu.VMEM((rows, cols), f32),
            pltpu.VMEM((rows, cols), f32),
            pltpu.VMEM((2, 3, side, side), bf16),
            pltpu.VMEM((side, side), bf16),
            pltpu.VMEM((4, 2, side, side), bf16),
            pltpu.VMEM((4, 2, side, side), f32),
            pltpu.VMEM((2, 8, cols), f32),
            pltpu.VMEM((2, 8, cols), f32),
            pltpu.VMEM((2, 8, cols), f32),
            pltpu.VMEM((8, cols), f32),
            pltpu.VMEM((8, cols), f32),
            pltpu.VMEM((n, 2, 8, 128), f32),
            pltpu.SMEM(block_plan.shape, jnp.int32),
            pltpu.VMEM((side, side), bf16),
            pltpu.SemaphoreType.DMA((2, 8)),
            pltpu.SemaphoreType.DMA((5,)),
            pltpu.SemaphoreType.DMA((9,)),
            pltpu.SemaphoreType.DMA((9,)),
            pltpu.SemaphoreType.DMA((n - 1,)),
            pltpu.SemaphoreType.DMA((n - 1,)),
        ],
        compiler_params=pltpu.CompilerParams(
            collective_id=0, has_side_effects=True, vmem_limit_bytes=56 * 1024 * 1024
        ),
        name="window",
    )(block_plan, smoother, surface, flux_x, flux_y, celerity, bed_depth, roughness)

    step = 32
    flat = pl.BlockSpec((step, cols), lambda i: (i, 0))
    new_surface, new_x, new_y, resident = pl.pallas_call(
        write_kernel,
        grid=(rows // step,),
        out_shape=(
            jax.ShapeDtypeStruct((rows, cols), f32),
            jax.ShapeDtypeStruct((rows, cols), f32),
            jax.ShapeDtypeStruct((rows, cols), f32),
            jax.ShapeDtypeStruct((3, 2, side, side), f32),
        ),
        in_specs=[
            smem,
            flat,
            pl.BlockSpec((4, 2, step, side), lambda i: (0, 0, i, 0)),
            pl.BlockSpec((2, 2, step, side), lambda i: (0, 0, i, 0)),
        ],
        out_specs=(flat, flat, flat, pl.BlockSpec((3, 2, step, side), lambda i: (0, 0, i, 0))),
        compiler_params=pltpu.CompilerParams(vmem_limit_bytes=56 * 1024 * 1024),
        name="write_out",
    )(block_plan, level, held, got)
    return new_surface, new_x, new_y, resident, energy


def solution(mesh):
    fields = P(("ens", "tile"), None)
    return jax.shard_map(
        on_device,
        mesh=mesh,
        in_specs=(fields,) * 6 + (P(), fields),
        out_specs=(fields, fields, fields, P(("ens", "tile"), None, None, None), P("ens")),
        check_vma=False,
    )
```

```python
import functools

import jax
import jax.numpy as jnp
from jax import lax
from jax.experimental import pallas as pl
from jax.experimental.pallas import tpu as pltpu
from jax.sharding import PartitionSpec as P

STEPS = 2
SUB = 12
STRIP = 16
MESH = pl.DeviceIdType.MESH


def window_kernel(
    n, plan_in, smoother_in, surface_in, flux_x_in, flux_y_in, celerity_in, bed_in, rough_in,
    level_out, held_out, got_out, energy_out,
    level, flux_x, flux_y, celerity, bed, rough, drag, turned, held, settled,
    below, above_level, above_flux, above_celerity, rim, shares,
    plan, s_ref, load_sem, store_sem, keep_sem, send_sem, recv_sem, share_send, share_recv,
):
    rows, cols = flux_y.shape
    side = s_ref.shape[0]
    blocks = cols // side
    half = cols // 2
    me = lax.axis_index("tile")
    ahead_tile = lax.rem(me + 1, n)
    behind_tile = lax.rem(me + n - 1, n)
    top = me == 0
    bottom = me == n - 1
    f32, bf16 = jnp.float32, jnp.bfloat16

    cut = rows // 2
    sources = (
        (surface_in, level, 0),
        (celerity_in, celerity, 0),
        (flux_x_in, flux_x, 8),
        (flux_y_in, flux_y, 0),
        (bed_in, bed, 0),
        (rough_in, rough, 0),
    )
    loads = [
        [
            pltpu.make_async_copy(
                source.at[pl.ds(part * cut, cut)], target.at[pl.ds(lead + part * cut, cut)], load_sem.at[part, i]
            )
            for i, (source, target, lead) in enumerate(sources)
        ]
        for part in range(2)
    ]
    loads[0] += [
        pltpu.make_async_copy(smoother_in, s_ref, load_sem.at[0, 6]),
        pltpu.make_async_copy(plan_in, plan, load_sem.at[0, 7]),
    ]
    for part in range(2):
        for load in loads[part]:
            load.start()

    barrier = pltpu.get_barrier_semaphore()

    def greet(d, _):
        pl.semaphore_signal(barrier, inc=1, device_id={"tile": lax.rem(me + d, n)}, device_id_type=MESH)
        return 0

    lax.fori_loop(1, n, greet, 0)
    pl.semaphore_wait(barrier, n - 1)

    def remote(source, target, index, device):
        return pltpu.make_async_remote_copy(
            src_ref=source, dst_ref=target, send_sem=send_sem.at[index], recv_sem=recv_sem.at[index],
            device_id={"tile": device}, device_id_type=MESH,
        )

    last = pl.ds(rows - 8, 8)
    up = [
        remote(surface_in.at[pl.ds(0, 8)], below.at[0], 0, behind_tile),
        remote(level.at[pl.ds(0, 8)], below.at[1], 1, behind_tile),
    ]
    down = [
        [
            remote(surface_in.at[last], above_level.at[0], 2, ahead_tile),
            remote(flux_x_in.at[last], above_flux.at[0], 3, ahead_tile),
            remote(celerity_in.at[last], above_celerity, 4, ahead_tile),
        ],
        [
            remote(level.at[last], above_level.at[1], 5, ahead_tile),
            remote(rim, above_flux.at[1], 6, ahead_tile),
        ],
    ]

    @pl.when(jnp.logical_not(top))
    def _():
        up[0].start()

    @pl.when(jnp.logical_not(bottom))
    def _():
        for copy in down[0]:
            copy.start()

    for load in loads[0]:
        load.wait()
    turned[...] = s_ref[...].astype(f32).T.astype(bf16)
    codes = [plan[0, c] for c in range(blocks)]

    def choose(options, matches):
        chosen = options[0]
        for option, match in zip(options[1:], matches[1:]):
            chosen = jnp.where(match, option, chosen)
        return chosen

    def with_code(wide, code):
        parts = [wide[:, c * side : (c + 1) * side] for c in range(blocks)]
        return choose(parts, [codes[c] == code for c in range(blocks)])

    def joined(which, at, size):
        options = [settled[code, which, pl.ds(at, size), :] for code in range(4)]
        return jnp.concatenate(
            [choose(options, [codes[c] == code for code in range(4)]) for c in range(blocks)], 1
        )

    col_ids = lax.broadcasted_iota(jnp.int32, (1, cols), 1)
    right_edge = lax.rem(col_ids, half) == half - 1
    left_edge = lax.rem(col_ids, half) == 0

    def strip_flux(step, which, at):
        if step == 0:
            return flux_x[pl.ds(8 + at, STRIP)] if which == 0 else flux_y[pl.ds(at, STRIP)]
        return joined(which, at, STRIP)

    def drag_of(at, new_level):
        ratio = rough[pl.ds(at, STRIP)] / jnp.maximum(new_level + bed[pl.ds(at, STRIP)], 1.0)
        ratio = ratio.astype(bf16)
        for code in range(1, 4):
            drag[0, code - 1, pl.ds(at, STRIP), :] = with_code(ratio, code)

    def advance(step):
        flux_x[pl.ds(0, 8)] = jnp.zeros((8, cols), f32)
        old_first = level[0:1]

        def strip(i, _):
            at = pl.multiple_of(i * STRIP, STRIP)
            now = level[pl.ds(at, STRIP)]
            after = level[pl.ds(at + STRIP, 8)]
            ahead = pltpu.roll(jnp.concatenate([now, after], 0), STRIP + 7, 0)[:STRIP]
            wave = celerity[pl.ds(at, STRIP)]
            new_x = strip_flux(step, 0, at) - wave * (ahead - now)
            right = jnp.where(right_edge, 0.0, pltpu.roll(now, cols - 1, 1))
            new_y = strip_flux(step, 1, at) - wave * (right - now)
            behind_x = pltpu.roll(jnp.concatenate([flux_x[pl.ds(at, 8)], new_x], 0), 1, 0)[8:]
            behind_y = jnp.where(left_edge, 0.0, pltpu.roll(new_y, 1, 1))
            new_level = now - (new_x - behind_x) - (new_y - behind_y)
            flux_x[pl.ds(8 + at, STRIP)] = new_x
            level[pl.ds(at, STRIP)] = new_level
            drag_of(at, new_level)
            for which, new in enumerate((new_x, new_y)):
                short = new.astype(bf16)
                for code in range(1, 4):
                    held[code, which, pl.ds(at, STRIP), :] = with_code(short, code)
                if step < STEPS - 1:
                    settled[0, which, pl.ds(at, STRIP), :] = with_code(new, 0)
                else:
                    held[0, which, pl.ds(at, STRIP), :] = with_code(short, 0)
            return 0

        count = rows // STRIP
        if step == 0:
            lax.fori_loop(0, count // 2 - 1, strip, 0)
            for load in loads[1]:
                load.wait()
            lax.fori_loop(count // 2 - 1, count - 1, strip, 0, unroll=2)
        else:
            lax.fori_loop(0, count - 1, strip, 0, unroll=3)

        @pl.when(bottom)
        def _():
            level[pl.ds(rows, 8)] = jnp.zeros((8, cols), f32)

        @pl.when(jnp.logical_not(bottom))
        def _():
            up[step].wait_recv()
            level[pl.ds(rows, 8)] = below[step]

        strip(count - 1, 0)

        @pl.when(jnp.logical_not(top))
        def _():
            for copy in down[step]:
                copy.wait_recv()
            above = above_flux[step] - above_celerity[...] * (old_first - above_level[step])
            first = lax.broadcasted_iota(jnp.int32, (8, 1), 0) == 0
            level[pl.ds(0, 8)] = level[pl.ds(0, 8)] + jnp.where(first, pltpu.roll(above, 1, 0), 0.0)
            drag_of(0, level[pl.ds(0, STRIP)])

    def settle(wanted, step):
        def product(pieces):
            tall = jnp.dot(
                jnp.concatenate(pieces, 0), turned[...], preferred_element_type=f32
            )
            return [tall[i * side : (i + 1) * side] for i in range(len(pieces))]

        def raw(flip):
            pieces = [held[code, which] for code, which in wanted]
            mixed = [piece.astype(bf16).T for piece in product(pieces)]
            return product(mixed)

        def repeat(flip):
            for i, value in enumerate(raw(flip)):
                weight = drag[flip, wanted[i][0] - 1]
                value = value.astype(bf16)
                held[wanted[i]] = value * pl.reciprocal(1 + weight * jnp.abs(value), approx=True)

        for code in sorted({code for code, _ in wanted}):
            drag[1, code - 1] = drag[0, code - 1].T

        def body(i, _):
            repeat(1)
            repeat(0)
            return 0

        lax.fori_loop(0, SUB // 2 - 1, body, 0)
        repeat(1)
        for i, value in enumerate(raw(0)):
            weight = drag[0, wanted[i][0] - 1].astype(f32)
            value = value / (1.0 + weight * jnp.abs(value))
            if step < STEPS - 1:
                settled[wanted[i]] = value
            held[wanted[i]] = value.astype(bf16)

    advance(0)
    for copy, edge in ((up[0], top), (down[0][0], bottom), (down[0][1], bottom), (down[0][2], bottom)):
        @pl.when(jnp.logical_not(edge))
        def _():
            copy.wait_send()

    @pl.when(jnp.logical_not(top))
    def _():
        up[1].start()

    @pl.when(jnp.logical_not(bottom))
    def _():
        down[1][0].start()

    settle([(code, which) for code in (1, 2, 3) for which in range(2)], 0)
    rim[...] = joined(0, rows - 8, 8)

    @pl.when(jnp.logical_not(top))
    def _():
        up[1].wait_send()

    @pl.when(jnp.logical_not(bottom))
    def _():
        down[1][1].start()
        down[1][0].wait_send()

    advance(1)

    total = n * rows

    def add_up(i, sums):
        at = pl.multiple_of(i * 8, 8)
        row = (me * rows + at + lax.broadcasted_iota(jnp.int32, (8, 1), 0)).astype(f32)
        value = level[pl.ds(at, 8)]
        return sums + (1.0 + 2.0 * row / total) * (value * value)

    sums = lax.fori_loop(0, rows // 8, add_up, jnp.zeros((8, cols), f32), unroll=4)
    for scenario in range(2):
        share = jnp.zeros((8, 128), f32)
        for c in range(half // 128):
            share = share + sums[:, scenario * half + c * 128 : scenario * half + (c + 1) * 128]
        shares[me, scenario] = share

    def spread(d, _):
        share_copy(d).start()
        return 0

    def share_copy(d):
        return pltpu.make_async_remote_copy(
            src_ref=shares.at[me], dst_ref=shares.at[me],
            send_sem=share_send.at[d - 1], recv_sem=share_recv.at[d - 1],
            device_id={"tile": lax.rem(me + d, n)}, device_id_type=MESH,
        )

    lax.fori_loop(1, n, spread, 0)
    keep_level = pltpu.make_async_copy(level.at[pl.ds(0, rows)], level_out, store_sem.at[0])
    keep_level.start()
    keep_dry = pltpu.make_async_copy(held.at[0], held_out.at[0], store_sem.at[4])
    keep_dry.start()

    sends = []
    keeps = [keep_dry]
    for group in (((3, 0), (3, 1), (2, 0)), ((2, 1), (1, 0), (1, 1))):
        settle(group, 1)
        for code, which in group:
            if code > 1:
                hop = code - 1
                send = remote(
                    held.at[code, which], got_out.at[hop - 1, which], 5 + 2 * hop + which, lax.rem(me + hop, n)
                )
                send.start()
                sends.append(send)
            keep = pltpu.make_async_copy(
                held.at[code, which], held_out.at[code, which], keep_sem.at[2 * code - 2 + which]
            )
            keep.start()
            keeps.append(keep)

    def gather(d, _):
        share_copy(d).wait()
        return 0

    lax.fori_loop(1, n, gather, 0)
    for scenario in range(2):
        def add_share(d, value):
            return value + shares[d, scenario]

        whole = lax.fori_loop(0, n, add_share, jnp.zeros((8, 128), f32))
        energy_out[scenario] = jnp.sum(whole) / (total * half)
    keep_level.wait()
    for keep in keeps:
        keep.wait()
    for send in sends:
        send.wait()

    @pl.when(jnp.logical_not(bottom))
    def _():
        down[1][1].wait_send()


def write_kernel(plan, level, held, got, level_out, flux_x_out, flux_y_out, resident_out):
    side = held.shape[-1]
    level_out[...] = level[...]
    for c in range(level.shape[1] // side):
        part = pl.ds(c * side, side)
        flux_x_out[:, part] = held[plan[0, c], 0].astype(jnp.float32)
        flux_y_out[:, part] = held[plan[0, c], 1].astype(jnp.float32)
    resident_out[0] = held[1].astype(jnp.float32)
    resident_out[1] = got[0].astype(jnp.float32)
    resident_out[2] = got[1].astype(jnp.float32)


def on_device(surface, flux_x, flux_y, celerity, bed_depth, roughness, smoother, block_plan):
    rows, cols = surface.shape
    side = smoother.shape[0]
    n = lax.axis_size("tile")
    f32, bf16 = jnp.float32, jnp.bfloat16
    whole = pl.BlockSpec(memory_space=pltpu.HBM)
    smem = pl.BlockSpec(memory_space=pltpu.SMEM)
    level, held, got, energy = pl.pallas_call(
        functools.partial(window_kernel, n),
        out_shape=(
            jax.ShapeDtypeStruct((rows, cols), f32),
            jax.ShapeDtypeStruct((4, 2, side, side), bf16),
            jax.ShapeDtypeStruct((2, 2, side, side), bf16),
            jax.ShapeDtypeStruct((2,), f32),
        ),
        in_specs=[whole] * 8,
        out_specs=(whole, whole, whole, smem),
        scratch_shapes=[
            pltpu.VMEM((rows + 8, cols), f32),
            pltpu.VMEM((rows + 8, cols), f32),
            pltpu.VMEM((rows, cols), f32),
            pltpu.VMEM((rows, cols), f32),
            pltpu.VMEM((rows, cols), f32),
            pltpu.VMEM((rows, cols), f32),
            pltpu.VMEM((2, 3, side, side), bf16),
            pltpu.VMEM((side, side), bf16),
            pltpu.VMEM((4, 2, side, side), bf16),
            pltpu.VMEM((4, 2, side, side), f32),
            pltpu.VMEM((2, 8, cols), f32),
            pltpu.VMEM((2, 8, cols), f32),
            pltpu.VMEM((2, 8, cols), f32),
            pltpu.VMEM((8, cols), f32),
            pltpu.VMEM((8, cols), f32),
            pltpu.VMEM((n, 2, 8, 128), f32),
            pltpu.SMEM(block_plan.shape, jnp.int32),
            pltpu.VMEM((side, side), bf16),
            pltpu.SemaphoreType.DMA((2, 8)),
            pltpu.SemaphoreType.DMA((5,)),
            pltpu.SemaphoreType.DMA((6,)),
            pltpu.SemaphoreType.DMA((11,)),
            pltpu.SemaphoreType.DMA((11,)),
            pltpu.SemaphoreType.DMA((n - 1,)),
            pltpu.SemaphoreType.DMA((n - 1,)),
        ],
        compiler_params=pltpu.CompilerParams(
            collective_id=0, has_side_effects=True, vmem_limit_bytes=56 * 1024 * 1024
        ),
        name="window",
    )(block_plan, smoother, surface, flux_x, flux_y, celerity, bed_depth, roughness)

    step = 128
    flat = pl.BlockSpec((step, cols), lambda i: (i, 0))
    new_surface, new_x, new_y, resident = pl.pallas_call(
        write_kernel,
        grid=(rows // step,),
        out_shape=(
            jax.ShapeDtypeStruct((rows, cols), f32),
            jax.ShapeDtypeStruct((rows, cols), f32),
            jax.ShapeDtypeStruct((rows, cols), f32),
            jax.ShapeDtypeStruct((3, 2, side, side), f32),
        ),
        in_specs=[
            smem,
            flat,
            pl.BlockSpec((4, 2, step, side), lambda i: (0, 0, i, 0)),
            pl.BlockSpec((2, 2, step, side), lambda i: (0, 0, i, 0)),
        ],
        out_specs=(flat, flat, flat, pl.BlockSpec((3, 2, step, side), lambda i: (0, 0, i, 0))),
        compiler_params=pltpu.CompilerParams(vmem_limit_bytes=56 * 1024 * 1024),
        name="write_out",
    )(block_plan, level, held, got)
    return new_surface, new_x, new_y, resident, energy


def solution(mesh):
    fields = P(("ens", "tile"), None)
    return jax.shard_map(
        on_device,
        mesh=mesh,
        in_specs=(fields,) * 6 + (P(), fields),
        out_specs=(fields, fields, fields, P(("ens", "tile"), None, None, None), P("ens")),
        check_vma=False,
    )
```

```python
import functools

import jax
import jax.numpy as jnp
from jax import lax
from jax.experimental import pallas as pl
from jax.experimental.pallas import tpu as pltpu
from jax.sharding import PartitionSpec as P

STEPS = 2
SUB = 12
STRIP = 16
MESH = pl.DeviceIdType.MESH


def window_kernel(
    n, plan_in, smoother_in, surface_in, flux_x_in, flux_y_in, celerity_in, bed_in, rough_in,
    level_out, held_out, got_out, energy_out,
    level, flux_x, flux_y, celerity, bed, rough, drag, turned, held, settled,
    below, above_level, above_flux, above_celerity, rim, shares,
    plan, s_ref, load_sem, store_sem, keep_sem, send_sem, recv_sem, share_send, share_recv,
):
    rows, cols = flux_y.shape
    side = s_ref.shape[0]
    blocks = cols // side
    half = cols // 2
    me = lax.axis_index("tile")
    ahead_tile = lax.rem(me + 1, n)
    behind_tile = lax.rem(me + n - 1, n)
    top = me == 0
    bottom = me == n - 1
    f32, bf16 = jnp.float32, jnp.bfloat16

    cut = rows // 2
    sources = (
        (surface_in, level, 0),
        (celerity_in, celerity, 0),
        (flux_x_in, flux_x, 8),
        (flux_y_in, flux_y, 0),
        (bed_in, bed, 0),
        (rough_in, rough, 0),
    )
    loads = [
        [
            pltpu.make_async_copy(
                source.at[pl.ds(part * cut, cut)], target.at[pl.ds(lead + part * cut, cut)], load_sem.at[part, i]
            )
            for i, (source, target, lead) in enumerate(sources)
        ]
        for part in range(2)
    ]
    loads[0] += [
        pltpu.make_async_copy(smoother_in, s_ref, load_sem.at[0, 6]),
        pltpu.make_async_copy(plan_in, plan, load_sem.at[0, 7]),
    ]
    for part in range(2):
        for load in loads[part]:
            load.start()

    barrier = pltpu.get_barrier_semaphore()

    def greet(d, _):
        pl.semaphore_signal(barrier, inc=1, device_id={"tile": lax.rem(me + d, n)}, device_id_type=MESH)
        return 0

    lax.fori_loop(1, n, greet, 0)
    pl.semaphore_wait(barrier, n - 1)

    def remote(source, target, index, device):
        return pltpu.make_async_remote_copy(
            src_ref=source, dst_ref=target, send_sem=send_sem.at[index], recv_sem=recv_sem.at[index],
            device_id={"tile": device}, device_id_type=MESH,
        )

    last = pl.ds(rows - 8, 8)
    up = [
        remote(surface_in.at[pl.ds(0, 8)], below.at[0], 0, behind_tile),
        remote(level.at[pl.ds(0, 8)], below.at[1], 1, behind_tile),
    ]
    down = [
        [
            remote(surface_in.at[last], above_level.at[0], 2, ahead_tile),
            remote(flux_x_in.at[last], above_flux.at[0], 3, ahead_tile),
            remote(celerity_in.at[last], above_celerity, 4, ahead_tile),
        ],
        [
            remote(level.at[last], above_level.at[1], 5, ahead_tile),
            remote(rim, above_flux.at[1], 6, ahead_tile),
        ],
    ]

    @pl.when(jnp.logical_not(top))
    def _():
        up[0].start()

    @pl.when(jnp.logical_not(bottom))
    def _():
        for copy in down[0]:
            copy.start()

    for load in loads[0]:
        load.wait()
    turned[...] = s_ref[...].astype(f32).T.astype(bf16)
    codes = [plan[0, c] for c in range(blocks)]

    def choose(options, matches):
        chosen = options[0]
        for option, match in zip(options[1:], matches[1:]):
            chosen = jnp.where(match, option, chosen)
        return chosen

    def with_code(wide, code):
        parts = [wide[:, c * side : (c + 1) * side] for c in range(blocks)]
        return choose(parts, [codes[c] == code for c in range(blocks)])

    def joined(which, at, size):
        options = [settled[code, which, pl.ds(at, size), :] for code in range(4)]
        return jnp.concatenate(
            [choose(options, [codes[c] == code for code in range(4)]) for c in range(blocks)], 1
        )

    col_ids = lax.broadcasted_iota(jnp.int32, (1, cols), 1)
    right_edge = lax.rem(col_ids, half) == half - 1
    left_edge = lax.rem(col_ids, half) == 0

    def strip_flux(step, which, at):
        if step == 0:
            return flux_x[pl.ds(8 + at, STRIP)] if which == 0 else flux_y[pl.ds(at, STRIP)]
        return joined(which, at, STRIP)

    def drag_of(at, new_level):
        ratio = rough[pl.ds(at, STRIP)] / jnp.maximum(new_level + bed[pl.ds(at, STRIP)], 1.0)
        ratio = ratio.astype(bf16)
        for code in range(1, 4):
            drag[0, code - 1, pl.ds(at, STRIP), :] = with_code(ratio, code)

    def advance(step):
        flux_x[pl.ds(0, 8)] = jnp.zeros((8, cols), f32)
        old_first = level[0:1]

        def strip(i, _):
            at = pl.multiple_of(i * STRIP, STRIP)
            now = level[pl.ds(at, STRIP)]
            after = level[pl.ds(at + STRIP, 8)]
            ahead = pltpu.roll(jnp.concatenate([now, after], 0), STRIP + 7, 0)[:STRIP]
            wave = celerity[pl.ds(at, STRIP)]
            new_x = strip_flux(step, 0, at) - wave * (ahead - now)
            right = jnp.where(right_edge, 0.0, pltpu.roll(now, cols - 1, 1))
            new_y = strip_flux(step, 1, at) - wave * (right - now)
            behind_x = pltpu.roll(jnp.concatenate([flux_x[pl.ds(at, 8)], new_x], 0), 1, 0)[8:]
            behind_y = jnp.where(left_edge, 0.0, pltpu.roll(new_y, 1, 1))
            new_level = now - (new_x - behind_x) - (new_y - behind_y)
            flux_x[pl.ds(8 + at, STRIP)] = new_x
            level[pl.ds(at, STRIP)] = new_level
            drag_of(at, new_level)
            for which, new in enumerate((new_x, new_y)):
                short = new.astype(bf16)
                for code in range(1, 4):
                    held[code, which, pl.ds(at, STRIP), :] = with_code(short, code)
                if step < STEPS - 1:
                    settled[0, which, pl.ds(at, STRIP), :] = with_code(new, 0)
                else:
                    held[0, which, pl.ds(at, STRIP), :] = with_code(short, 0)
            return 0

        count = rows // STRIP
        if step == 0:
            lax.fori_loop(0, count // 2 - 1, strip, 0)
            for load in loads[1]:
                load.wait()
            lax.fori_loop(count // 2 - 1, count - 1, strip, 0, unroll=2)
        else:
            lax.fori_loop(0, count - 1, strip, 0, unroll=3)

        @pl.when(bottom)
        def _():
            level[pl.ds(rows, 8)] = jnp.zeros((8, cols), f32)

        @pl.when(jnp.logical_not(bottom))
        def _():
            up[step].wait_recv()
            level[pl.ds(rows, 8)] = below[step]

        strip(count - 1, 0)

        @pl.when(jnp.logical_not(top))
        def _():
            for copy in down[step]:
                copy.wait_recv()
            above = above_flux[step] - above_celerity[...] * (old_first - above_level[step])
            first = lax.broadcasted_iota(jnp.int32, (8, 1), 0) == 0
            level[pl.ds(0, 8)] = level[pl.ds(0, 8)] + jnp.where(first, pltpu.roll(above, 1, 0), 0.0)
            drag_of(0, level[pl.ds(0, STRIP)])

    def settle(wanted, step):
        def product(pieces):
            tall = jnp.dot(
                jnp.concatenate(pieces, 0), turned[...], preferred_element_type=f32
            )
            return [tall[i * side : (i + 1) * side] for i in range(len(pieces))]

        def raw(flip):
            pieces = [held[code, which] for code, which in wanted]
            mixed = [piece.astype(bf16).T for piece in product(pieces)]
            return product(mixed)

        def repeat(flip):
            for i, value in enumerate(raw(flip)):
                weight = drag[flip, wanted[i][0] - 1]
                value = value.astype(bf16)
                held[wanted[i]] = value * pl.reciprocal(1 + weight * jnp.abs(value), approx=True)

        for code in sorted({code for code, _ in wanted}):
            drag[1, code - 1] = drag[0, code - 1].T

        def body(i, _):
            repeat(1)
            repeat(0)
            return 0

        lax.fori_loop(0, SUB // 2 - 1, body, 0)
        repeat(1)
        for i, value in enumerate(raw(0)):
            weight = drag[0, wanted[i][0] - 1].astype(f32)
            value = value / (1.0 + weight * jnp.abs(value))
            if step < STEPS - 1:
                settled[wanted[i]] = value
            held[wanted[i]] = value.astype(bf16)

    advance(0)
    for copy, edge in ((up[0], top), (down[0][0], bottom), (down[0][1], bottom), (down[0][2], bottom)):
        @pl.when(jnp.logical_not(edge))
        def _():
            copy.wait_send()

    @pl.when(jnp.logical_not(top))
    def _():
        up[1].start()

    @pl.when(jnp.logical_not(bottom))
    def _():
        down[1][0].start()

    settle([(code, which) for code in (1, 2, 3) for which in range(2)], 0)
    rim[...] = joined(0, rows - 8, 8)

    @pl.when(jnp.logical_not(top))
    def _():
        up[1].wait_send()

    @pl.when(jnp.logical_not(bottom))
    def _():
        down[1][1].start()
        down[1][0].wait_send()

    advance(1)

    total = n * rows

    def add_up(i, sums):
        at = pl.multiple_of(i * 8, 8)
        row = (me * rows + at + lax.broadcasted_iota(jnp.int32, (8, 1), 0)).astype(f32)
        value = level[pl.ds(at, 8)]
        return sums + (1.0 + 2.0 * row / total) * (value * value)

    sums = lax.fori_loop(0, rows // 8, add_up, jnp.zeros((8, cols), f32), unroll=4)
    for scenario in range(2):
        share = jnp.zeros((8, 128), f32)
        for c in range(half // 128):
            share = share + sums[:, scenario * half + c * 128 : scenario * half + (c + 1) * 128]
        shares[me, scenario] = share

    def spread(d, _):
        share_copy(d).start()
        return 0

    def share_copy(d):
        return pltpu.make_async_remote_copy(
            src_ref=shares.at[me], dst_ref=shares.at[me],
            send_sem=share_send.at[d - 1], recv_sem=share_recv.at[d - 1],
            device_id={"tile": lax.rem(me + d, n)}, device_id_type=MESH,
        )

    lax.fori_loop(1, n, spread, 0)
    keep_level = pltpu.make_async_copy(level.at[pl.ds(0, rows)], level_out, store_sem.at[0])
    keep_level.start()
    keep_dry = pltpu.make_async_copy(held.at[0], held_out.at[0], store_sem.at[4])
    keep_dry.start()

    sends = []
    keeps = [keep_dry]
    for group in (((3, 0), (3, 1), (2, 0)), ((2, 1), (1, 0), (1, 1))):
        settle(group, 1)
        for code, which in group:
            if code > 1:
                hop = code - 1
                send = remote(
                    held.at[code, which], got_out.at[hop - 1, which], 5 + 2 * hop + which, lax.rem(me + hop, n)
                )
                send.start()
                sends.append(send)
            keep = pltpu.make_async_copy(
                held.at[code, which], held_out.at[code, which], keep_sem.at[2 * code - 2 + which]
            )
            keep.start()
            keeps.append(keep)

    def gather(d, _):
        share_copy(d).wait()
        return 0

    lax.fori_loop(1, n, gather, 0)
    for scenario in range(2):
        def add_share(d, value):
            return value + shares[d, scenario]

        whole = lax.fori_loop(0, n, add_share, jnp.zeros((8, 128), f32))
        energy_out[scenario] = jnp.sum(whole) / (total * half)
    keep_level.wait()
    for keep in keeps:
        keep.wait()
    for send in sends:
        send.wait()

    @pl.when(jnp.logical_not(bottom))
    def _():
        down[1][1].wait_send()


def write_kernel(plan, level, held, got, level_out, flux_x_out, flux_y_out, resident_out):
    side = held.shape[-1]
    level_out[...] = level[...]
    for c in range(level.shape[1] // side):
        part = pl.ds(c * side, side)
        flux_x_out[:, part] = held[plan[0, c], 0].astype(jnp.float32)
        flux_y_out[:, part] = held[plan[0, c], 1].astype(jnp.float32)
    resident_out[0] = held[1].astype(jnp.float32)
    resident_out[1] = got[0].astype(jnp.float32)
    resident_out[2] = got[1].astype(jnp.float32)


def on_device(surface, flux_x, flux_y, celerity, bed_depth, roughness, smoother, block_plan):
    rows, cols = surface.shape
    side = smoother.shape[0]
    n = lax.axis_size("tile")
    f32, bf16 = jnp.float32, jnp.bfloat16
    whole = pl.BlockSpec(memory_space=pltpu.HBM)
    smem = pl.BlockSpec(memory_space=pltpu.SMEM)
    level, held, got, energy = pl.pallas_call(
        functools.partial(window_kernel, n),
        out_shape=(
            jax.ShapeDtypeStruct((rows, cols), f32),
            jax.ShapeDtypeStruct((4, 2, side, side), bf16),
            jax.ShapeDtypeStruct((2, 2, side, side), bf16),
            jax.ShapeDtypeStruct((2,), f32),
        ),
        in_specs=[whole] * 8,
        out_specs=(whole, whole, whole, smem),
        scratch_shapes=[
            pltpu.VMEM((rows + 8, cols), f32),
            pltpu.VMEM((rows + 8, cols), f32),
            pltpu.VMEM((rows, cols), f32),
            pltpu.VMEM((rows, cols), f32),
            pltpu.VMEM((rows, cols), f32),
            pltpu.VMEM((rows, cols), f32),
            pltpu.VMEM((2, 3, side, side), bf16),
            pltpu.VMEM((side, side), bf16),
            pltpu.VMEM((4, 2, side, side), bf16),
            pltpu.VMEM((4, 2, side, side), f32),
            pltpu.VMEM((2, 8, cols), f32),
            pltpu.VMEM((2, 8, cols), f32),
            pltpu.VMEM((2, 8, cols), f32),
            pltpu.VMEM((8, cols), f32),
            pltpu.VMEM((8, cols), f32),
            pltpu.VMEM((n, 2, 8, 128), f32),
            pltpu.SMEM(block_plan.shape, jnp.int32),
            pltpu.VMEM((side, side), bf16),
            pltpu.SemaphoreType.DMA((2, 8)),
            pltpu.SemaphoreType.DMA((5,)),
            pltpu.SemaphoreType.DMA((6,)),
            pltpu.SemaphoreType.DMA((11,)),
            pltpu.SemaphoreType.DMA((11,)),
            pltpu.SemaphoreType.DMA((n - 1,)),
            pltpu.SemaphoreType.DMA((n - 1,)),
        ],
        compiler_params=pltpu.CompilerParams(
            collective_id=0, has_side_effects=True, vmem_limit_bytes=56 * 1024 * 1024
        ),
        name="window",
    )(block_plan, smoother, surface, flux_x, flux_y, celerity, bed_depth, roughness)

    step = rows
    flat = pl.BlockSpec((step, cols), lambda i: (i, 0))
    new_surface, new_x, new_y, resident = pl.pallas_call(
        write_kernel,
        grid=(rows // step,),
        out_shape=(
            jax.ShapeDtypeStruct((rows, cols), f32),
            jax.ShapeDtypeStruct((rows, cols), f32),
            jax.ShapeDtypeStruct((rows, cols), f32),
            jax.ShapeDtypeStruct((3, 2, side, side), f32),
        ),
        in_specs=[
            smem,
            flat,
            pl.BlockSpec((4, 2, step, side), lambda i: (0, 0, i, 0)),
            pl.BlockSpec((2, 2, step, side), lambda i: (0, 0, i, 0)),
        ],
        out_specs=(flat, flat, flat, pl.BlockSpec((3, 2, step, side), lambda i: (0, 0, i, 0))),
        compiler_params=pltpu.CompilerParams(vmem_limit_bytes=56 * 1024 * 1024),
        name="write_out",
    )(block_plan, level, held, got)
    return new_surface, new_x, new_y, resident, energy


def solution(mesh):
    fields = P(("ens", "tile"), None)
    return jax.shard_map(
        on_device,
        mesh=mesh,
        in_specs=(fields,) * 6 + (P(), fields),
        out_specs=(fields, fields, fields, P(("ens", "tile"), None, None, None), P("ens")),
        check_vma=False,
    )
```
